32 devices in a mesh: pair: 16 (over z, x, core), row: 2 (over y).
Axes of the slice: x: 2, y: 2, z: 4, core: 2. Of those that a mesh axis runs over, the one named last changes fastest.
Arguments:
- gram_field: float32 [64, 2, 16, 16, 256], P('pair', None, 'row'), may hold values from -3.6 to 3.6, as said below
- left_variance: float32 [64, 16, 16], P('pair'), may hold values from 0.25 to 4
- right_variance: float32 [2, 16, 16], replicated, may hold values from 0.25 to 4
- cotangent: float32 [64, 2, 8, 8, 64], P('pair', 'row'), may hold values from -24 to 24
Outputs:
- gram_gradient: float32 [64, 2, 16, 16, 256], P('pair', None, 'row')
- left_gradient: float32 [64, 16, 16], P('pair')
- right_gradient: float32 [2, 16, 16], replicated
The draws below stay inside these ranges and needn't reach their ends.
Inputs may be any that keep to these rules, and one draw needn't show every extreme that they name: `gram_field`: each entry lies within 0.9 times the square root of the product of left_variance and right_variance at its two pixels.
All inputs are finite; a program needn't handle non-finite values.
Results may differ from the reference program's by a relative error of at most 0.00008.
Values sent between devices are 32-bit elements; how exact they have to be, the bound alone decides.
A program may use at most 64 MiB of HBM per device.

```python
import math
import jax
import jax.numpy as jnp
from jax import lax

R = 16
H = 8
A = 64
B = 2


def shared_variances(key):
    key_left = jax.random.fold_in(key, 11)
    key_right = jax.random.fold_in(key, 12)
    low = math.log(0.25)
    high = math.log(4.0)
    left = jnp.exp(jax.random.uniform(key_left, (A, R, R), jnp.float32, low, high))
    right = jnp.exp(jax.random.uniform(key_right, (B, R, R), jnp.float32, low, high))
    return (left, right)


def draw_left_variance(key, part):
    return shared_variances(key)[0]


def draw_right_variance(key, part):
    return shared_variances(key)[1]


def draw_gram_field(key, part):
    left, right = shared_variances(key)
    key_ratio = jax.random.fold_in(key, 13)
    ratio = jax.random.uniform(key_ratio, (A, B, R, R, R * R), jnp.float32, -0.9, 0.9)
    left_root = jnp.sqrt(left)[:, None, :, :, None]
    right_root = jnp.sqrt(right).reshape(1, B, 1, 1, R * R)
    return left_root * right_root * ratio


def shard_levels(key, shape, cuts, smallest, largest):
    def one(dim, shards_of):
        draws = jax.random.uniform(jax.random.fold_in(jax.random.fold_in(key, 6), dim), (shards_of,), jnp.float32, smallest / len(cuts), largest / len(cuts))
        return jnp.repeat(jnp.exp(draws), shape[dim] // shards_of).reshape((-1,) + (1,) * (len(shape) - dim - 1))

    factor_of = one(*cuts[0])
    for cut in cuts[1:]:
        factor_of = factor_of * one(*cut)
    return factor_of


def scatter_about(key, dims, width, bound, split=(), held_as=jnp.bfloat16):
    array = width * jax.random.normal(key, dims, jnp.float32)
    if split:
        array = array * shard_levels(key, dims, split, -0.22, 0.18)
    return jnp.clip(array, -bound, bound).astype(held_as)


def setup_inputs(seed: int = 0) -> dict:
    seeds = jax.random.split(jax.random.key(seed), 5)
    gram_field = draw_gram_field(jax.random.fold_in(seeds[4], 71), 0)
    left_variance = draw_left_variance(jax.random.fold_in(seeds[4], 71), 0)
    right_variance = draw_right_variance(jax.random.fold_in(seeds[4], 71), 0)
    cotangent = scatter_about(seeds[3], (A, B, H, H, H * H), 4.0, 24.0, ((0, 16), (1, 2)), jnp.float32)
    return dict(gram_field=gram_field, left_variance=left_variance, right_variance=right_variance, cotangent=cotangent)


def shifted(source, dimension, offset):
    dimension = dimension % source.ndim
    extent = source.shape[dimension]
    margin = abs(offset)
    widths = [(0, 0)] * source.ndim
    widths[dimension] = (margin, margin)
    padded = jnp.pad(source, widths)
    return lax.slice_in_dim(padded, margin + offset, margin + offset + extent, axis=dimension)

def column_masks(length):
    column_index = jnp.arange(length * length) % length
    return ((column_index + 1 < length).astype(jnp.float32), (column_index >= 1).astype(jnp.float32))

def mix_columns(source, length):
    mask_up, mask_down = column_masks(length)
    return source + shifted(shifted(source, -2, 1), -1, 1) * mask_up + shifted(shifted(source, -2, -1), -1, -1) * mask_down

def conv_field(padded, length):
    inner = padded[..., 1:-1, :, :] + shifted(padded[..., 2:, :, :], -1, length) + shifted(padded[..., :-2, :, :], -1, -length)
    return mix_columns(inner, length) / 9.0

def pad_rows(source):
    widths = [(0, 0)] * source.ndim
    widths[source.ndim - 3] = (1, 1)
    return jnp.pad(source, widths)

def conv_map(source):
    row_sum = source + shifted(source, -2, 1) + shifted(source, -2, -1)
    return (row_sum + shifted(row_sum, -1, 1) + shifted(row_sum, -1, -1)) / 9.0

def pool_field(source):
    shape = source.shape
    leading = shape[:-3]
    count = shape[-3]
    length = shape[-2]
    half_side = length // 2
    merged = source.reshape(shape[:-1] + (half_side, 2 * length))
    merged = merged[..., :length] + merged[..., length:]
    merged = merged.reshape(shape[:-1] + (half_side * length,))
    merged = merged[..., 0::2] + merged[..., 1::2]
    merged = merged.reshape(leading + (count // 2, 2, half_side, 2, half_side * half_side))
    return lax.optimization_barrier(jnp.sum(merged, axis=(-4, -2))) / 16.0

def spread_field(source):
    half_side = source.shape[-2]
    merged = jnp.repeat(source, 2, axis=-3)
    merged = jnp.repeat(merged, 2, axis=-2)
    inner = merged.shape[:-1]
    merged = merged.reshape(inner + (half_side, 1, half_side, 1))
    merged = jnp.broadcast_to(merged, inner + (half_side, 2, half_side, 2))
    return merged.reshape(inner + (4 * half_side * half_side,)) / 16.0

def pool_map(source):
    extent = source.shape[-1] // 2
    merged = source.reshape(source.shape[:-2] + (extent, 2, extent, 2))
    return lax.optimization_barrier(jnp.mean(merged, axis=(-3, -1)))

def spread_map(source):
    return jnp.repeat(jnp.repeat(source, 2, axis=-2), 2, axis=-1) / 4.0

def arc_kernel(source, left, right):
    magnitude = jnp.sqrt(left * right)
    cosine = source / magnitude
    angle_part = jnp.pi - jnp.arccos(cosine)
    sine_part = jnp.sqrt(1.0 - cosine * cosine)
    kernel = magnitude * (sine_part + angle_part * cosine) / (2.0 * jnp.pi)
    slopes = angle_part / (2.0 * jnp.pi)
    weights = magnitude * sine_part / (4.0 * jnp.pi)
    return (kernel, slopes, weights)

def reference(gram_field, left_variance, right_variance, cotangent):
    length = gram_field.shape[3]
    half_side = length // 2
    count = right_variance.shape[0]
    first_right = conv_map(right_variance)
    right_flat = first_right.reshape(count, 1, 1, length * length)
    second_right = conv_map(pool_map(first_right / 2.0))
    second_flat = second_right.reshape(count, 1, 1, half_side * half_side)

    def one_image(items):
        gram_one, variance_one, cot_one = items
        first_left = conv_map(variance_one)
        source_one = conv_field(pad_rows(gram_one), length)
        kernel_one, slope_one, weight_one = arc_kernel(source_one, first_left[None, :, :, None], right_flat)
        second_left = conv_map(pool_map(first_left / 2.0))
        source_two = conv_field(pad_rows(pool_field(kernel_one)), half_side)
        unused, slope_two, weight_two = arc_kernel(source_two, second_left[None, :, :, None], second_flat)
        weighted_two = cot_one * weight_two
        left_two = lax.optimization_barrier(jnp.sum(weighted_two, axis=(0, 3))) / second_left
        right_two = lax.optimization_barrier(jnp.sum(weighted_two, axis=(1, 2))) / second_flat.reshape(count, half_side * half_side)
        back_one = spread_field(conv_field(pad_rows(cot_one * slope_two), half_side))
        weighted_one = back_one * weight_one
        left_one = spread_map(conv_map(left_two)) / 2.0 + lax.optimization_barrier(jnp.sum(weighted_one, axis=(0, 3))) / first_left
        right_local = lax.optimization_barrier(jnp.sum(weighted_one, axis=(1, 2))) / right_flat.reshape(count, length * length)
        right_one = spread_map(conv_map(right_two.reshape(count, half_side, half_side))) / 2.0 + right_local.reshape(count, length, length)
        gram_grad = conv_field(pad_rows(back_one * slope_one), length)
        return (gram_grad, conv_map(left_one), right_one)
    gram_gradient, left_gradient, right_parts = lax.map(one_image, (gram_field, left_variance, cotangent))
    right_gradient = conv_map(lax.optimization_barrier(jnp.sum(right_parts, axis=0)))
    return (gram_gradient, left_gradient, right_gradient)
```

```python
import functools
import math

import jax
import jax.numpy as jnp
import numpy as np
from jax import lax
from jax.experimental import pallas as pl
from jax.experimental.pallas import tpu as pltpu
from jax.sharding import PartitionSpec as P

ARCSIN_EVEN = (2.61397078, -1.36807576, 0.342139678, -0.0179491288)
ARCSIN_ROOT = (-1.61397053, 0.727749535, -0.104947558)


def conv_map(source):
    padded = jnp.pad(source, ((0, 0), (1, 1), (1, 1)))
    n = source.shape[-1]
    rows = padded[:, 0:n] + padded[:, 1 : n + 1] + padded[:, 2 : n + 2]
    return (rows[:, :, 0:n] + rows[:, :, 1 : n + 1] + rows[:, :, 2 : n + 2]) / 9.0


def pool_map(source):
    extent = source.shape[-1] // 2
    merged = source.reshape(source.shape[:-2] + (extent, 2, extent, 2))
    return jnp.mean(merged, axis=(-3, -1))


def spread_map(source):
    return jnp.repeat(jnp.repeat(source, 2, axis=-2), 2, axis=-1) / 4.0


def pool_matrices(length, group):
    half = length // 2
    width = half * half
    matrix = np.zeros((group, length * length, group * width), np.float32)
    for k in range(length):
        for l in range(length):
            for b in range(group):
                matrix[b, k * length + l, b * width + (k // 2) * half + l // 2] = 1.0
    return jnp.asarray(matrix, jnp.bfloat16)


def split_dot(x, matrix, dims):
    high = x.astype(jnp.bfloat16)
    low = (x - high.astype(jnp.float32)).astype(jnp.bfloat16)
    dot = functools.partial(
        lax.dot_general, dimension_numbers=(dims, ((), ())), preferred_element_type=jnp.float32
    )
    return dot(high, matrix) + dot(low, matrix)


def arc_parts(rho):
    square = rho * rho
    rest = 1.0 - square
    sine = rest * lax.rsqrt(rest)
    even = ARCSIN_EVEN[3]
    for c in ARCSIN_EVEN[2::-1]:
        even = even * square + c
    root = ARCSIN_ROOT[2]
    for c in ARCSIN_ROOT[1::-1]:
        root = root * square + c
    angle = (0.5 * math.pi) + rho * (even + sine * root)
    return sine, angle


def lane_masks(shape, side):
    lane = lax.broadcasted_iota(jnp.int32, shape, 1)
    sub = lax.broadcasted_iota(jnp.int32, shape, 0)
    col = lax.rem(lane, side)
    k = lax.rem(lane // side, side)
    k_up = k + 1 < side
    k_down = k >= 1
    v_up = (col + 1 < side) & (sub + 1 < shape[0])
    v_down = (col >= 1) & (sub >= 1)
    return k_up, k_down, v_up, v_down


def roll(x, shift, axis):
    return pltpu.roll(x, shift % x.shape[axis], axis)


def conv_rows(rows, side, masks):
    k_up, k_down, v_up, v_down = masks
    out = []
    for i in range(1, len(rows) - 1):
        inner = rows[i]
        if rows[i + 1] is not None:
            inner = inner + jnp.where(k_up, roll(rows[i + 1], -side, 1), 0.0)
        if rows[i - 1] is not None:
            inner = inner + jnp.where(k_down, roll(rows[i - 1], side, 1), 0.0)
        up = jnp.where(v_up, roll(roll(inner, -1, 0), -1, 1), 0.0)
        down = jnp.where(v_down, roll(roll(inner, 1, 0), 1, 1), 0.0)
        out.append(inner + up + down)
    return out


def body(
    sizes,
    gram_hbm, cot_hbm, gl_ref, il_ref, gr_ref, ir_ref, gl2_ref, il2_ref, gr2_ref, ir2_ref, mat_ref,
    out_hbm, left_out, right_out, left2_out,
    gram, cot, slope, sinem, kp, tmp, pooled, back, fine, wsum, wsum2, racc, out_v, left_all, pair_all, packet,
    load_sem, out_sem, halo_send, halo_recv, cot_send, cot_recv, pool_send, pool_recv,
    slope_send, slope_recv, left_send, left_recv, pair_send, pair_recv,
):
    n, npair, A, B, rows, R, group, part = sizes
    H = R // 2
    W = R * R
    G = B // group
    PR = rows // 2
    width = H * H
    me = lax.axis_index("row")
    mine = lax.axis_index("pair")

    loads = []
    for a in range(A):
        c = pltpu.make_async_copy(gram_hbm.at[a], gram.at[a, :, pl.ds(1, rows)], load_sem.at[a])
        c.start()
        loads.append(c)
    cot_load = pltpu.make_async_copy(cot_hbm, cot.at[me], load_sem.at[A])
    cot_load.start()

    barrier = pltpu.get_barrier_semaphore()
    for d in range(1, n):
        pl.semaphore_signal(barrier, inc=1, device_id={"row": lax.rem(me + d, n)})
    for d in range(1, npair):
        pl.semaphore_signal(barrier, inc=1, device_id={"pair": lax.rem(mine + d, npair)})
    pl.semaphore_wait(barrier, n - 1 + npair - 1)

    has_low = me > 0
    has_high = me < n - 1
    low = jnp.maximum(me - 1, 0)
    high = jnp.minimum(me + 1, n - 1)

    def halo_up():
        return pltpu.make_async_remote_copy(
            src_ref=gram_hbm.at[:, :, rows - 1], dst_ref=gram.at[:, :, 0],
            send_sem=halo_send.at[0], recv_sem=halo_recv.at[0], device_id={"row": high})

    def halo_down():
        return pltpu.make_async_remote_copy(
            src_ref=gram_hbm.at[:, :, 0], dst_ref=gram.at[:, :, rows + 1],
            send_sem=halo_send.at[1], recv_sem=halo_recv.at[1], device_id={"row": low})

    def slope_up():
        return pltpu.make_async_remote_copy(
            src_ref=slope.at[:, :, rows], dst_ref=slope.at[:, :, 0],
            send_sem=slope_send.at[0], recv_sem=slope_recv.at[0], device_id={"row": high})

    def slope_down():
        return pltpu.make_async_remote_copy(
            src_ref=slope.at[:, :, 1], dst_ref=slope.at[:, :, rows + 1],
            send_sem=slope_send.at[1], recv_sem=slope_recv.at[1], device_id={"row": low})

    def row_copy(ref, sends, recvs, d):
        return pltpu.make_async_remote_copy(
            src_ref=ref.at[me], dst_ref=ref.at[me], send_sem=sends.at[d],
            recv_sem=recvs.at[me], device_id={"row": lax.rem(me + d, n)})

    def row_arrival(ref, sends, recvs, d):
        source = lax.rem(me + d, n)
        return pltpu.make_async_remote_copy(
            src_ref=ref.at[source], dst_ref=ref.at[source], send_sem=sends.at[d],
            recv_sem=recvs.at[source], device_id={"row": source})

    @pl.when(has_high)
    def _():
        halo_up().start()

    @pl.when(has_low)
    def _():
        halo_down().start()

    zero_row = jnp.zeros((A, B, R, W), jnp.float32)

    @pl.when(jnp.logical_not(has_low))
    def _():
        gram[:, :, 0] = zero_row
        slope[:, :, 0] = zero_row

    @pl.when(jnp.logical_not(has_high))
    def _():
        gram[:, :, rows + 1] = zero_row
        slope[:, :, rows + 1] = zero_row

    cot_load.wait()
    for d in range(1, n):
        row_copy(cot, cot_send, cot_recv, d).start()
    for c in loads:
        c.wait()

    masks = lane_masks((R, W), R)

    def forward(a, b, p):
        f = [gram[a, b, 2 * p + t] for t in range(4)]
        source = conv_rows(f, R, masks)
        total = None
        for t in range(2):
            i = 2 * p + t
            gl = gl_ref[a, i]
            il = il_ref[a, i]
            gl = jnp.concatenate([gl] * (W // 128), axis=1)
            il = jnp.concatenate([il] * (W // 128), axis=1)
            m = gl * gr_ref[b][None, :]
            rho = source[t] * (il * ir_ref[b][None, :])
            sine, angle = arc_parts(rho)
            sm = m * sine
            slope[a, b, i + 1] = angle
            sinem[a, b, i] = sm
            term = sm + m * (angle * rho)
            total = term if total is None else total + term
        kp[a, b, p] = total

    interior = list(range(1, PR - 1))
    edges = sorted({0, PR - 1})

    if interior:
        @pl.loop(0, A)
        def _(a):
            for b in range(B):
                for p in interior:
                    forward(a, b, p)

    @pl.when(has_low)
    def _():
        halo_up().wait_recv()

    @pl.when(has_high)
    def _():
        halo_down().wait_recv()

    @pl.loop(0, A)
    def _(a):
        for b in range(B):
            for p in edges:
                forward(a, b, p)
        for g in range(G):
            acc = None
            for t in range(group):
                x = kp[a, g * group + t].reshape(PR * R, W)
                y = split_dot(x, mat_ref[t], ((1,), (0,)))
                acc = y if acc is None else acc + y
            tmp[g] = acc
            even = tmp[g, pl.ds(0, PR * H, stride=2), :]
            odd = tmp[g, pl.ds(1, PR * H, stride=2), :]
            pooled[me, a, g] = ((even + odd) * (1.0 / (32.0 * math.pi))).reshape(PR, H, 128)

    for d in range(1, n):
        row_copy(pooled, pool_send, pool_recv, d).start()

    @pl.when(has_high)
    def _():
        slope_up().start()

    @pl.when(has_low)
    def _():
        slope_down().start()

    for d in range(1, n):
        row_arrival(cot, cot_send, cot_recv, d).wait_recv()
    for d in range(1, n):
        row_arrival(pooled, pool_send, pool_recv, d).wait_recv()

    masks2 = lane_masks((H, 128), H)
    for g in range(G):
        racc[2 * B + g] = jnp.zeros((R, 128), jnp.float32)

    @pl.loop(0, A)
    def _(a):
        left2 = [None] * H
        for g in range(G):
            f = [None] + [pooled[i // PR, a, g, i % PR] for i in range(H)] + [None]
            source = conv_rows(f, H, masks2)
            ct = [None]
            right2 = None
            for i in range(H):
                m = gl2_ref[a, i] * gr2_ref[g][None, :]
                rho = source[i] * (il2_ref[a, i] * ir2_ref[g][None, :])
                sine, angle = arc_parts(rho)
                pieces = []
                for t in range(group):
                    b = g * group + t
                    pieces.append(cot[b // part, a, b % part, i])
                c = jnp.concatenate(pieces, axis=1)
                ct.append(c * angle)
                w = c * (m * sine)
                right2 = w if right2 is None else right2 + w
                left2[i] = w if left2[i] is None else left2[i] + w
            ct.append(None)
            racc[2 * B + g, 0:H] = racc[2 * B + g, 0:H] + right2
            b_rows = conv_rows(ct, H, masks2)
            scale = 1.0 / (9.0 * 2.0 * math.pi * 16.0) / (18.0 * math.pi)
            zero = jnp.zeros((H, 128), jnp.float32)
            back[g, 0] = zero
            back[g, H + 1] = zero
            for i in range(H):
                back[g, i + 1] = b_rows[i] * scale
            x = back[g, pl.ds(me * PR, PR + 2)].reshape((PR + 2) * H, 128)
            for t in range(group):
                y = split_dot(x, mat_ref[t], ((1,), (1,)))
                for h in range(W // 128):
                    part_y = y[:, h * 128 : (h + 1) * 128]
                    fine[a, g * group + t, h, pl.ds(0, (PR + 2) * H, stride=2), :] = part_y
                    fine[a, g * group + t, h, pl.ds(1, (PR + 2) * H, stride=2), :] = part_y
        for i in range(H):
            wsum2[a, i] = left2[i]

    def back_row(a, b, c):
        return jnp.concatenate([fine[a, b, h, c * R : (c + 1) * R, :] for h in range(W // 128)], axis=1)

    racc[0 : 2 * B] = jnp.zeros((2 * B, R, 128), jnp.float32)

    @pl.loop(0, A)
    def _(a):
        lsum = [None] * rows
        for b in range(B):
            total = None
            for p in range(PR):
                bk = back_row(a, b, p + 1)
                for t in range(2):
                    i = 2 * p + t
                    w = bk * sinem[a, b, i]
                    total = w if total is None else total + w
                    lsum[i] = w if lsum[i] is None else lsum[i] + w
            for h in range(W // 128):
                racc[2 * b + h] = racc[2 * b + h] + total[:, h * 128 : (h + 1) * 128]
        for i in range(rows):
            wsum[a, i] = lsum[i]

    ones_bf = jnp.ones((8, W), jnp.bfloat16)

    def lane_sums(x):
        high_part = x.astype(jnp.bfloat16)
        low_part = (x - high_part.astype(jnp.float32)).astype(jnp.bfloat16)
        dims = (((1,), (1,)), ((), ()))
        ones = ones_bf[:, : x.shape[1]]
        return lax.dot_general(ones, high_part, dims, preferred_element_type=jnp.float32) + lax.dot_general(
            ones, low_part, dims, preferred_element_type=jnp.float32)

    nl = A * rows * R // 128
    ls = lane_sums(wsum[...].reshape(A * rows * R, W))
    for c in range(nl):
        left_all[me, 2 * B + G + c : 2 * B + G + c + 1, :] = ls[0:1, c * 128 : (c + 1) * 128]
    left_all[me, 0 : 2 * B + G, :] = jnp.sum(racc[...], axis=1)
    for d in range(1, n):
        row_copy(left_all, left_send, left_recv, d).start()

    ls2 = lane_sums(wsum2[...].reshape(A * H * H, 128))
    for c in range(A * H * H // 128):
        left2_out[c : c + 1, :] = ls2[0:1, c * 128 : (c + 1) * 128]

    def final(a, b, chosen):
        cache = {}

        def product(i):
            if i not in cache:
                cache[i] = back_row(a, b, (i + 1) // 2) * slope[a, b, i]
            return cache[i]

        for i in chosen:
            (value,) = conv_rows([product(i - 1), product(i), product(i + 1)], R, masks)
            out_v[a, b, i - 1] = value

    if rows > 2:
        @pl.loop(0, A)
        def _(a):
            for b in range(B):
                final(a, b, range(2, rows))

    for d in range(1, n):
        row_arrival(left_all, left_send, left_recv, d).wait_recv()
    left_out[...] = left_all[...]
    right = left_all[0, 0 : 2 * B, :]
    for r in range(1, n):
        right = right + left_all[r, 0 : 2 * B, :]
    packet_rows = packet.shape[0]
    packet[...] = jnp.zeros((packet_rows, 128), jnp.float32)
    packet[0 : 2 * B, :] = right
    packet[2 * B : 2 * B + G, :] = left_all[me, 2 * B : 2 * B + G, :]
    pair_all[mine] = packet[...]

    def pair_copy(d):
        return pltpu.make_async_remote_copy(
            src_ref=packet, dst_ref=pair_all.at[mine], send_sem=pair_send.at[d],
            recv_sem=pair_recv.at[mine], device_id={"pair": lax.rem(mine + d, npair)})

    def pair_arrival(d):
        source = lax.rem(mine + d, npair)
        return pltpu.make_async_remote_copy(
            src_ref=packet, dst_ref=pair_all.at[source], send_sem=pair_send.at[d],
            recv_sem=pair_recv.at[source], device_id={"pair": source})

    for d in range(1, npair):
        pair_copy(d).start()

    @pl.when(has_low)
    def _():
        slope_up().wait_recv()

    @pl.when(has_high)
    def _():
        slope_down().wait_recv()

    @pl.loop(0, A)
    def _(a):
        for b in range(B):
            final(a, b, sorted({1, rows}))
        pltpu.make_async_copy(out_v.at[a], out_hbm.at[a], out_sem.at[a]).start()

    for d in range(1, npair):
        pair_arrival(d).wait_recv()
    total = pair_all[0]
    for r in range(1, npair):
        total = total + pair_all[r]
    right_out[...] = total

    for a in range(A):
        pltpu.make_async_copy(out_v.at[a], out_hbm.at[a], out_sem.at[a]).wait()

    @pl.when(has_high)
    def _():
        halo_up().wait_send()
        slope_up().wait_send()

    @pl.when(has_low)
    def _():
        halo_down().wait_send()
        slope_down().wait_send()

    for d in range(1, n):
        row_copy(cot, cot_send, cot_recv, d).wait_send()
        row_copy(pooled, pool_send, pool_recv, d).wait_send()
        row_copy(left_all, left_send, left_recv, d).wait_send()
    for d in range(1, npair):
        pair_copy(d).wait_send()


def on_device(n, npair, gram_field, left_variance, right_variance, cotangent):
    A, B, rows, R, W = gram_field.shape
    part = cotangent.shape[1]
    H = R // 2
    width = H * H
    group = 128 // width
    G = B // group
    PR = rows // 2
    rank = lax.axis_index("row")
    start = rank * rows
    f32 = jnp.float32

    first_left = conv_map(left_variance)
    first_right = conv_map(right_variance)
    second_left = conv_map(pool_map(first_left / 2.0))
    second_right = conv_map(pool_map(first_right / 2.0))
    my_left = lax.dynamic_slice_in_dim(first_left, start, rows, axis=1)
    gl = jnp.broadcast_to(jnp.sqrt(my_left)[..., None], (A, rows, R, 128))
    il = jnp.broadcast_to((lax.rsqrt(my_left) / 9.0)[..., None], (A, rows, R, 128))
    gl2 = jnp.broadcast_to(jnp.sqrt(second_left)[..., None], (A, H, H, 128))
    il2 = jnp.broadcast_to((lax.rsqrt(second_left) / 9.0)[..., None], (A, H, H, 128))
    gr = jnp.sqrt(first_right).reshape(B, W)
    ir = lax.rsqrt(first_right).reshape(B, W)
    gr2 = jnp.sqrt(second_right).reshape(G, 128)
    ir2 = lax.rsqrt(second_right).reshape(G, 128)
    mats = pool_matrices(R, group)

    nl = A * rows * R // 128
    left_rows = -(-(2 * B + G + nl) // 8) * 8
    pair_rows = -(-(2 * B + G) // 8) * 8
    sizes = (n, npair, A, B, rows, R, group, part)
    vmem = pl.BlockSpec(memory_space=pltpu.VMEM)
    hbm = pl.BlockSpec(memory_space=pl.ANY)
    dma = pltpu.SemaphoreType.DMA
    out, left, right, left2 = pl.pallas_call(
        functools.partial(body, sizes),
        out_shape=(
            jax.ShapeDtypeStruct(gram_field.shape, f32),
            jax.ShapeDtypeStruct((n, left_rows, 128), f32),
            jax.ShapeDtypeStruct((pair_rows, 128), f32),
            jax.ShapeDtypeStruct((A * H * H // 128, 128), f32),
        ),
        in_specs=[hbm, hbm] + [vmem] * 9,
        out_specs=(hbm, vmem, vmem, vmem),
        scratch_shapes=[
            pltpu.VMEM((A, B, rows + 2, R, W), f32),
            pltpu.VMEM((n, A, part, H, H, width), f32),
            pltpu.VMEM((A, B, rows + 2, R, W), f32),
            pltpu.VMEM((A, B, rows, R, W), f32),
            pltpu.VMEM((A, B, PR, R, W), f32),
            pltpu.VMEM((G, PR * R, 128), f32),
            pltpu.VMEM((n, A, G, PR, H, 128), f32),
            pltpu.VMEM((G, H + 2, H, 128), f32),
            pltpu.VMEM((A, B, W // 128, (PR + 2) * R, 128), f32),
            pltpu.VMEM((A, rows, R, W), f32),
            pltpu.VMEM((A, H, H, 128), f32),
            pltpu.VMEM((2 * B + G, R, 128), f32),
            pltpu.VMEM((A, B, rows, R, W), f32),
            pltpu.VMEM((n, left_rows, 128), f32),
            pltpu.VMEM((npair, pair_rows, 128), f32),
            pltpu.VMEM((pair_rows, 128), f32),
            dma((A + 1,)), dma((A,)), dma((2,)), dma((2,)),
            dma((n,)), dma((n,)), dma((n,)), dma((n,)),
            dma((2,)), dma((2,)), dma((n,)), dma((n,)), dma((npair,)), dma((npair,)),
        ],
        compiler_params=pltpu.CompilerParams(
            collective_id=0, has_side_effects=True, vmem_limit_bytes=48 * 1024 * 1024
        ),
        name="arc_reverse",
    )(gram_field, cotangent, gl, il, gr, ir, gl2, il2, gr2, ir2, mats)

    left_sum = left[:, 2 * B + G : 2 * B + G + nl].reshape(n, A, rows, R)
    left_sum = left_sum.transpose(1, 0, 2, 3).reshape(A, n * rows, R) * 4.5
    left_two = left2.reshape(A, H, H) / (4.0 * math.pi) / second_left
    left_one = spread_map(conv_map(left_two)) / 2.0 + left_sum / first_left
    right_sum = right[: 2 * B].reshape(B, R, R) * 4.5
    right_two = right[2 * B : 2 * B + G].reshape(B, H, H) / (4.0 * math.pi) / second_right
    right_one = spread_map(conv_map(right_two)) / 2.0 + right_sum / first_right
    return out, conv_map(left_one), conv_map(right_one)


def solution(mesh):
    in_specs = (
        P("pair", None, "row", None, None),
        P("pair", None, None),
        P(),
        P("pair", "row", None, None, None),
    )
    out_specs = (P("pair", None, "row", None, None), P("pair", None, None), P())
    return jax.shard_map(
        functools.partial(on_device, mesh.shape["row"], mesh.shape["pair"]),
        mesh=mesh, in_specs=in_specs, out_specs=out_specs, check_vma=False,
    )
```

```python
import functools
import math

import jax
import jax.numpy as jnp
from jax import lax
from jax.experimental import pallas as pl
from jax.experimental.pallas import tpu as pltpu
from jax.sharding import PartitionSpec as P

ARCSIN_EVEN = (2.61397078, -1.36807576, 0.342139678, -0.0179491288)
ARCSIN_ROOT = (-1.61397053, 0.727749535, -0.104947558)


def divided(x, k):
    return x >> (k.bit_length() - 1) if k & (k - 1) == 0 else lax.div(x, k)


def left_over(x, k):
    return x & (k - 1) if k & (k - 1) == 0 else lax.rem(x, k)


def lane_of(shape):
    return lax.broadcasted_iota(jnp.int32, shape, len(shape) - 1)


def sub_of(shape):
    return lax.broadcasted_iota(jnp.int32, shape, len(shape) - 2)


def pool_matrix(length, group, t):
    half = length // 2
    shape = (length * length, group * half * half)
    row = sub_of(shape)
    lane = lane_of(shape)
    row_k, row_l = divided(row, length), left_over(row, length)
    lane_t, place = divided(lane, half * half), left_over(lane, half * half)
    same = (
        (lane_t == t)
        & (divided(row_k, 2) == divided(place, half))
        & (divided(row_l, 2) == left_over(place, half))
    )
    return jnp.where(same, 1.0, 0.0).astype(jnp.bfloat16)


def split_dot(x, matrix, dims=((1,), (0,)), terms=2):
    total = None
    for _ in range(terms):
        piece = x.astype(jnp.bfloat16)
        y = lax.dot_general(piece, matrix, (dims, ((), ())), preferred_element_type=jnp.float32)
        total = y if total is None else total + y
        x = x - piece.astype(jnp.float32)
    return total


def arc_parts(rho):
    square = rho * rho
    rest = 1.0 - square
    sine = rest * lax.rsqrt(rest)
    even = ARCSIN_EVEN[3]
    for c in ARCSIN_EVEN[2::-1]:
        even = even * square + c
    root = ARCSIN_ROOT[2]
    for c in ARCSIN_ROOT[1::-1]:
        root = root * square + c
    angle = (0.5 * math.pi) + rho * (even + sine * root)
    return sine, angle


def roll(x, shift, axis):
    return pltpu.roll(x, shift % x.shape[axis], axis)


def lane_masks(shape, side, chunks):
    lane = lane_of(shape)
    sub = sub_of(shape)
    col = left_over(lane, side)
    if chunks > 1:
        k_up, k_down = lane < 128 - side, lane >= side
    else:
        k = left_over(divided(lane, side), side)
        k_up, k_down = k + 1 < side, k >= 1
    l_up, l_down = col + 1 < side, col >= 1
    return k_up, k_down, l_up, l_down, l_up & (sub + 1 < shape[0]), l_down & (sub >= 1)


def shift_k_up(chunks, side, mask):
    rolled = [roll(c, -side, 1) for c in chunks] + [0.0]
    return [jnp.where(mask, rolled[h], rolled[h + 1]) for h in range(len(chunks))]


def shift_k_down(chunks, side, mask):
    rolled = [0.0] + [roll(c, side, 1) for c in chunks]
    return [jnp.where(mask, rolled[h + 1], rolled[h]) for h in range(len(chunks))]


def conv_rows(rows, side, masks):
    k_up, k_down, _, _, v_up, v_down = masks
    out = []
    for i in range(1, len(rows) - 1):
        inner = rows[i]
        if rows[i + 1] is not None:
            inner = [x + y for x, y in zip(inner, shift_k_up(rows[i + 1], side, k_up))]
        if rows[i - 1] is not None:
            inner = [x + y for x, y in zip(inner, shift_k_down(rows[i - 1], side, k_down))]
        done = []
        for x in inner:
            up = jnp.where(v_up, roll(roll(x, -1, 0), -1, 1), 0.0)
            down = jnp.where(v_down, roll(roll(x, 1, 0), 1, 1), 0.0)
            done.append(x + up + down)
        out.append(done)
    return out


def conv_flat(chunks, side, masks):
    k_up, k_down, l_up, l_down, _, _ = masks
    ups = shift_k_up(chunks, side, k_up)
    downs = shift_k_down(chunks, side, k_down)
    out = []
    for x, up, down in zip(chunks, ups, downs):
        x = x + up + down
        x = x + jnp.where(l_up, roll(x, -1, 1), 0.0) + jnp.where(l_down, roll(x, 1, 1), 0.0)
        out.append(x * (1.0 / 9.0))
    return out


def conv_columns(columns):
    count, extent = columns.shape[0], columns.shape[1]
    sub = sub_of((extent, 128))
    out = []
    for i in range(count):
        x = columns[i]
        if i > 0:
            x = x + columns[i - 1]
        if i + 1 < count:
            x = x + columns[i + 1]
        up = jnp.where(sub + 1 < extent, roll(x, -1, 0), 0.0)
        down = jnp.where(sub >= 1, roll(x, 1, 0), 0.0)
        out.append((x + up + down) * (1.0 / 9.0))
    return out


def root_pair(x):
    inverse = lax.rsqrt(x)
    return x * inverse, inverse


def rounded(count):
    return -(-count // 8) * 8


def body(
    sizes,
    gram_hbm, cot_hbm, lv_ref, rv_ref,
    out_hbm, left_out, right_out,
    gram, cot, slope, sinem, kp, tmp, pooled, back, fine, wsum, wsum2, racc, out_v, packet, pair_all, pair_packet,
    gl_ref, il_ref, gl2_ref, il2_ref, gr_ref, ir_ref, gr2_ref, ir2_ref, mat_ref, lmap, cols, half_cols, ccol,
    load_sem, out_sem, halo_send, halo_recv, cot_send, cot_recv, pool_send, pool_recv,
    slope_send, slope_recv, left_send, left_recv, pair_send, pair_recv,
):
    n, npair, A, B, rows, R, group, part = sizes
    H = R // 2
    W = R * R
    NH = W // 128
    G = B // group
    PR = rows // 2
    Bp = rounded(B)
    Gp = rounded(G)
    LR = A * rows
    me = lax.axis_index("row")
    mine = lax.axis_index("pair")
    f32 = jnp.float32

    def chunk(h):
        return slice(h * 128, (h + 1) * 128)

    barrier = pltpu.get_barrier_semaphore()
    for d in range(1, n):
        pl.semaphore_signal(barrier, inc=1, device_id={"row": lax.rem(me + d, n)})
    for d in range(1, npair):
        pl.semaphore_signal(barrier, inc=1, device_id={"pair": lax.rem(mine + d, npair)})

    loads = []
    for a in range(A):
        c = pltpu.make_async_copy(gram_hbm.at[a], gram.at[a, :, pl.ds(1, rows)], load_sem.at[a])
        c.start()
        loads.append(c)
    cot_load = pltpu.make_async_copy(cot_hbm, cot.at[me], load_sem.at[A])
    cot_load.start()

    pl.semaphore_wait(barrier, n - 1 + npair - 1)

    has_low = me > 0
    has_high = me < n - 1
    low = jnp.maximum(me - 1, 0)
    high = jnp.minimum(me + 1, n - 1)

    def halo_up():
        return pltpu.make_async_remote_copy(
            src_ref=gram_hbm.at[:, :, rows - 1], dst_ref=gram.at[:, :, 0],
            send_sem=halo_send.at[0], recv_sem=halo_recv.at[0], device_id={"row": high})

    def halo_down():
        return pltpu.make_async_remote_copy(
            src_ref=gram_hbm.at[:, :, 0], dst_ref=gram.at[:, :, rows + 1],
            send_sem=halo_send.at[1], recv_sem=halo_recv.at[1], device_id={"row": low})

    def slope_up():
        return pltpu.make_async_remote_copy(
            src_ref=slope.at[:, :, rows], dst_ref=slope.at[:, :, 0],
            send_sem=slope_send.at[0], recv_sem=slope_recv.at[0], device_id={"row": high})

    def slope_down():
        return pltpu.make_async_remote_copy(
            src_ref=slope.at[:, :, 1], dst_ref=slope.at[:, :, rows + 1],
            send_sem=slope_send.at[1], recv_sem=slope_recv.at[1], device_id={"row": low})

    def row_copy(ref, sends, recvs, d):
        return pltpu.make_async_remote_copy(
            src_ref=ref.at[me], dst_ref=ref.at[me], send_sem=sends.at[d],
            recv_sem=recvs.at[me], device_id={"row": lax.rem(me + d, n)})

    def row_arrival(ref, sends, recvs, d):
        source = lax.rem(me + d, n)
        return pltpu.make_async_remote_copy(
            src_ref=ref.at[source], dst_ref=ref.at[source], send_sem=sends.at[d],
            recv_sem=recvs.at[source], device_id={"row": source})

    def pool_copy(d, a):
        return pltpu.make_async_remote_copy(
            src_ref=pooled.at[me, a], dst_ref=pooled.at[me, a], send_sem=pool_send.at[d, a],
            recv_sem=pool_recv.at[me, a], device_id={"row": lax.rem(me + d, n)})

    def pool_arrival(d, a):
        source = lax.rem(me + d, n)
        return pltpu.make_async_remote_copy(
            src_ref=pooled.at[source, a], dst_ref=pooled.at[source, a], send_sem=pool_send.at[d, a],
            recv_sem=pool_recv.at[source, a], device_id={"row": source})

    @pl.when(has_high)
    def _():
        halo_up().start()

    @pl.when(has_low)
    def _():
        halo_down().start()

    cot_load.wait()
    for d in range(1, n):
        row_copy(cot, cot_send, cot_recv, d).start()

    zero_row = jnp.zeros((A, B, R, W), f32)

    @pl.when(jnp.logical_not(has_low))
    def _():
        gram[:, :, 0] = zero_row
        slope[:, :, 0] = zero_row

    @pl.when(jnp.logical_not(has_high))
    def _():
        gram[:, :, rows + 1] = zero_row
        slope[:, :, rows + 1] = zero_row

    for t in range(group):
        mat_ref[t] = pool_matrix(R, group, t)
    ones = jnp.ones((128, 128), jnp.bfloat16)
    lmap[...] = jnp.zeros((A, R, 128), f32)
    lmap[:, :, 0:R] = lv_ref[...]
    sub16 = sub_of((R, 128))
    lane16 = lane_of((R, 128))
    band = jnp.abs(sub16 - lane16) <= 1
    for a in range(A):
        v = lmap[a]
        v = v + jnp.where(sub16 + 1 < R, roll(v, -1, 0), 0.0) + jnp.where(sub16 >= 1, roll(v, 1, 0), 0.0)
        lmap[a] = v
        for i in range(R):
            line = jnp.broadcast_to(lmap[a, i : i + 1, :], (R, 128))
            cols[a, i] = jnp.where(band, line, 0.0)
        spread = split_dot(cols[a].reshape(R * R, 128), ones, terms=3) * (1.0 / 9.0)
        cols[a] = spread.reshape(R, R, 128)
        for c in range(H):
            half_cols[a, c * R : (c + 1) * R] = cols[a, 2 * c] + cols[a, 2 * c + 1]
        even = half_cols[a, pl.ds(0, H * H, stride=2), :]
        odd = half_cols[a, pl.ds(1, H * H, stride=2), :]
        second = conv_columns(((even + odd) * 0.125).reshape(H, H, 128))
        for i in range(H):
            g2, i2 = root_pair(second[i])
            gl2_ref[a, i] = g2
            il2_ref[a, i] = i2 * (1.0 / 9.0)
        g1, i1 = root_pair(cols[a, pl.ds(me * rows, rows)])
        gl_ref[a] = g1
        il_ref[a] = i1 * (1.0 / 9.0)

    flat_masks = lane_masks((Bp, 128), R, NH)
    flat_masks2 = lane_masks((Gp, 128), H, 1)
    first_right = conv_flat([rv_ref[:, chunk(h)] for h in range(NH)], R, flat_masks)
    for h in range(NH):
        gr_ref[:, chunk(h)], ir_ref[:, chunk(h)] = root_pair(first_right[h])
    first_flat = jnp.concatenate(first_right, axis=1)
    small = [split_dot(first_flat, mat_ref[t], terms=3) for t in range(group)]
    gr2_ref[...] = jnp.ones((Gp, 128), f32)
    for g in range(G):
        line = None
        for t in range(group):
            b = g * group + t
            y = small[t][b : b + 1, :]
            line = y if line is None else line + y
        gr2_ref[g : g + 1, :] = line * 0.125
    (second_right,) = conv_flat([gr2_ref[...]], H, flat_masks2)
    gr2_ref[...], ir2_ref[...] = root_pair(second_right)

    for c in loads:
        c.wait()

    masks = lane_masks((R, 128), R, NH)

    def forward(a, b, p):
        f = [[gram[a, b, 2 * p + t, :, chunk(h)] for h in range(NH)] for t in range(4)]
        source = conv_rows(f, R, masks)
        for h in range(NH):
            total = None
            for t in range(2):
                i = 2 * p + t
                m = gl_ref[a, i] * gr_ref[b : b + 1, chunk(h)]
                rho = source[t][h] * (il_ref[a, i] * ir_ref[b : b + 1, chunk(h)])
                sine, angle = arc_parts(rho)
                sm = m * sine
                slope[a, b, i + 1, :, chunk(h)] = angle
                sinem[a, b, i, :, chunk(h)] = sm
                term = sm + m * (angle * rho)
                total = term if total is None else total + term
            kp[a, b, p, :, chunk(h)] = total

    interior = list(range(1, PR - 1))
    edges = sorted({0, PR - 1})

    if interior:
        @pl.loop(0, A)
        def _(a):
            for b in range(B):
                for p in interior:
                    forward(a, b, p)

    @pl.when(has_low)
    def _():
        halo_up().wait_recv()

    @pl.when(has_high)
    def _():
        halo_down().wait_recv()

    @pl.loop(0, A)
    def _(a):
        for b in range(B):
            for p in edges:
                forward(a, b, p)
        for g in range(G):
            acc = None
            for t in range(group):
                y = split_dot(kp[a, g * group + t].reshape(PR * R, W), mat_ref[t])
                acc = y if acc is None else acc + y
            tmp[g, 0 : PR * R] = acc
            even = tmp[g, pl.ds(0, PR * H, stride=2), :]
            odd = tmp[g, pl.ds(1, PR * H, stride=2), :]
            pooled[me, a, g] = ((even + odd) * (1.0 / (32.0 * math.pi))).reshape(PR, H, 128)
        for d in range(1, n):
            pool_copy(d, a).start()

    @pl.when(has_high)
    def _():
        slope_up().start()

    @pl.when(has_low)
    def _():
        slope_down().start()

    for d in range(1, n):
        row_arrival(cot, cot_send, cot_recv, d).wait_recv()

    masks2 = lane_masks((H, 128), H, 1)
    racc[...] = jnp.zeros((NH * B + G, R, 128), f32)

    @pl.loop(0, A)
    def _(a):
        for d in range(1, n):
            pool_arrival(d, a).wait_recv()
        left2 = [None] * H
        for g in range(G):
            f = [None] + [[pooled[i // PR, a, g, i % PR]] for i in range(H)] + [None]
            source = conv_rows(f, H, masks2)
            ct = [None]
            right2 = None
            for i in range(H):
                m = gl2_ref[a, i] * gr2_ref[g : g + 1, :]
                rho = source[i][0] * (il2_ref[a, i] * ir2_ref[g : g + 1, :])
                sine, angle = arc_parts(rho)
                pieces = []
                for t in range(group):
                    b = g * group + t
                    pieces.append(cot[b // part, a, b % part, i])
                c = jnp.concatenate(pieces, axis=1)
                ct.append([c * angle])
                w = c * (m * sine)
                right2 = w if right2 is None else right2 + w
                left2[i] = w if left2[i] is None else left2[i] + w
            ct.append(None)
            racc[NH * B + g, 0:H] = racc[NH * B + g, 0:H] + right2
            b_rows = conv_rows(ct, H, masks2)
            scale = 1.0 / (9.0 * 2.0 * math.pi * 16.0) / (18.0 * math.pi)
            zero = jnp.zeros((H, 128), f32)
            back[g, 0] = zero
            back[g, H + 1] = zero
            for i in range(H):
                back[g, i + 1] = b_rows[i][0] * scale
            x = back[g, pl.ds(me * PR, PR + 2)].reshape((PR + 2) * H, 128)
            for t in range(group):
                y = split_dot(x, mat_ref[t], ((1,), (1,)))
                for h in range(NH):
                    fine[a, g * group + t, h, pl.ds(0, (PR + 2) * H, stride=2), :] = y[:, chunk(h)]
                    fine[a, g * group + t, h, pl.ds(1, (PR + 2) * H, stride=2), :] = y[:, chunk(h)]
        for i in range(H):
            wsum2[a, i] = left2[i]

        lsum = [None] * rows
        for b in range(B):
            for h in range(NH):
                total = None
                for p in range(PR):
                    bk = fine[a, b, h, (p + 1) * R : (p + 2) * R, :]
                    for t in range(2):
                        i = 2 * p + t
                        w = bk * sinem[a, b, i, :, chunk(h)]
                        total = w if total is None else total + w
                        lsum[i] = w if lsum[i] is None else lsum[i] + w
                racc[h * B + b] = racc[h * B + b] + total
        for i in range(rows):
            wsum[a, i] = lsum[i]

    diagonal = (sub16 == lane16)[None]
    sums = split_dot(wsum[...].reshape(LR * R, 128), ones).reshape(LR, R, 128)
    inverse = il_ref[...].reshape(LR, R, 128)
    sums = sums * (inverse * inverse * (4.5 * 81.0))
    packet[me, 0:LR, :] = jnp.sum(jnp.where(diagonal, sums, 0.0), axis=1)
    right_sums = jnp.sum(racc[...], axis=1)
    packet[me, LR : LR + NH * B, :] = right_sums[0 : NH * B]
    for d in range(1, n):
        row_copy(packet, left_send, left_recv, d).start()

    def final(a, b, chosen):
        cache = {}

        def product(i):
            if i not in cache:
                c = (i + 1) // 2
                cache[i] = [
                    fine[a, b, h, c * R : (c + 1) * R, :] * slope[a, b, i, :, chunk(h)] for h in range(NH)
                ]
            return cache[i]

        for i in chosen:
            (value,) = conv_rows([product(i - 1), product(i), product(i + 1)], R, masks)
            for h in range(NH):
                out_v[a, b, i - 1, :, chunk(h)] = value[h]

    def inner_out(a):
        inner = pl.ds(1, rows - 2)
        return pltpu.make_async_copy(out_v.at[a, :, inner], out_hbm.at[a, :, inner], out_sem.at[0, a])

    def edge_out(a, i, s):
        return pltpu.make_async_copy(out_v.at[a, :, i], out_hbm.at[a, :, i], out_sem.at[s, a])

    if rows > 2:
        @pl.loop(0, A)
        def _(a):
            for b in range(B):
                final(a, b, range(2, rows))
            inner_out(a).start()

    for d in range(1, n):
        row_arrival(packet, left_send, left_recv, d).wait_recv()
    right = packet[0, LR : LR + NH * B, :]
    for r in range(1, n):
        right = right + packet[r, LR : LR + NH * B, :]
    pair_packet[...] = jnp.zeros(pair_packet.shape, f32)
    pair_packet[0 : NH * B, :] = right
    pair_packet[NH * B : NH * B + G, :] = right_sums[NH * B : NH * B + G]
    pair_all[mine] = pair_packet[...]

    def pair_copy(d):
        return pltpu.make_async_remote_copy(
            src_ref=pair_packet, dst_ref=pair_all.at[mine], send_sem=pair_send.at[d],
            recv_sem=pair_recv.at[mine], device_id={"pair": lax.rem(mine + d, npair)})

    def pair_arrival(d):
        source = lax.rem(mine + d, npair)
        return pltpu.make_async_remote_copy(
            src_ref=pair_packet, dst_ref=pair_all.at[source], send_sem=pair_send.at[d],
            recv_sem=pair_recv.at[source], device_id={"pair": source})

    for d in range(1, npair):
        pair_copy(d).start()

    @pl.when(has_low)
    def _():
        slope_up().wait_recv()

    @pl.when(has_high)
    def _():
        slope_down().wait_recv()

    @pl.loop(0, A)
    def _(a):
        for b in range(B):
            final(a, b, sorted({1, rows}))
        edge_out(a, 0, 1).start()
        edge_out(a, rows - 1, 2).start()

    inverse2 = il2_ref[...].reshape(A * H, H, 128)
    sums2 = split_dot(wsum2[...].reshape(A * H * H, 128), ones).reshape(A * H, H, 128)
    sums2 = sums2 * (inverse2 * inverse2 * (81.0 / (4.0 * math.pi * 8.0)))
    for a in range(A):
        mixed = conv_columns(sums2[a * H : (a + 1) * H])
        for c in range(H):
            for t in range(2):
                ccol[pl.ds((2 * c + t) * R, H, stride=2), :] = mixed[c]
                ccol[pl.ds((2 * c + t) * R + 1, H, stride=2), :] = mixed[c]
        coarse = jnp.sum(jnp.where(diagonal, ccol[...].reshape(R, R, 128), 0.0), axis=1)
        local = jnp.concatenate([packet[r, a * rows : (a + 1) * rows, :] for r in range(n)], axis=0)
        v = coarse + local
        v = v + jnp.where(sub16 + 1 < R, roll(v, -1, 0), 0.0) + jnp.where(sub16 >= 1, roll(v, 1, 0), 0.0)
        v = (v + roll(v, 1, 1) + roll(v, -1, 1)) * (1.0 / 9.0)
        left_out[a] = v[:, 0:R]

    for d in range(1, npair):
        pair_arrival(d).wait_recv()
    total = pair_all[0]
    for r in range(1, npair):
        total = total + pair_all[r]
    pair_packet_rows = pair_packet.shape[0]
    tmp[0, 0:pair_packet_rows, :] = total
    tmp[0, pair_packet_rows : pair_packet_rows + Gp, :] = jnp.zeros((Gp, 128), f32)
    coarse = tmp[0, NH * B : NH * B + Gp, :]
    (coarse,) = conv_flat([coarse * (ir2_ref[...] * ir2_ref[...] * (1.0 / (4.0 * math.pi * 8.0)))], H, flat_masks2)
    wide = [split_dot(coarse, mat_ref[t], ((1,), (1,)), terms=3) for t in range(group)]
    for b in range(B):
        right_out[b : b + 1, :] = wide[b % group][b // group : b // group + 1, :]
    if Bp > B:
        right_out[B:Bp, :] = jnp.zeros((Bp - B, W), f32)
    pieces = []
    for h in range(NH):
        scale = ir_ref[:, chunk(h)]
        pieces.append(right_out[:, chunk(h)] + tmp[0, h * B : h * B + Bp, :] * (scale * scale * 4.5))
    pieces = conv_flat(pieces, R, flat_masks)
    for h in range(NH):
        right_out[:, chunk(h)] = pieces[h]

    for a in range(A):
        if rows > 2:
            inner_out(a).wait()
        edge_out(a, 0, 1).wait()
        edge_out(a, rows - 1, 2).wait()

    @pl.when(has_high)
    def _():
        halo_up().wait_send()
        slope_up().wait_send()

    @pl.when(has_low)
    def _():
        halo_down().wait_send()
        slope_down().wait_send()

    for d in range(1, n):
        row_copy(cot, cot_send, cot_recv, d).wait_send()
        row_copy(packet, left_send, left_recv, d).wait_send()
        for a in range(A):
            pool_copy(d, a).wait_send()
    for d in range(1, npair):
        pair_copy(d).wait_send()


def on_device(n, npair, gram_field, left_variance, right_variance, cotangent):
    A, B, rows, R, W = gram_field.shape
    part = cotangent.shape[1]
    H = R // 2
    NH = W // 128
    width = H * H
    group = 128 // width
    G = B // group
    PR = rows // 2
    Bp, Gp = rounded(B), rounded(G)
    f32 = jnp.float32
    right_flat = jnp.pad(right_variance.reshape(B, W), ((0, Bp - B), (0, 0)), constant_values=1.0)

    pair_rows = rounded(NH * B + G)
    packet_rows = rounded(A * rows + NH * B)
    sizes = (n, npair, A, B, rows, R, group, part)
    vmem = pl.BlockSpec(memory_space=pltpu.VMEM)
    hbm = pl.BlockSpec(memory_space=pl.ANY)
    dma = pltpu.SemaphoreType.DMA

    def scratch(*shape):
        return pltpu.VMEM(shape, f32)

    out, left, right = pl.pallas_call(
        functools.partial(body, sizes),
        out_shape=(
            jax.ShapeDtypeStruct(gram_field.shape, f32),
            jax.ShapeDtypeStruct((A, R, R), f32),
            jax.ShapeDtypeStruct((Bp, W), f32),
        ),
        in_specs=[hbm, hbm, vmem, vmem],
        out_specs=(hbm, vmem, vmem),
        scratch_shapes=[
            scratch(A, B, rows + 2, R, W),
            scratch(n, A, part, H, H, width),
            scratch(A, B, rows + 2, R, W),
            scratch(A, B, rows, R, W),
            scratch(A, B, PR, R, W),
            scratch(G, max(PR * R, pair_rows + Gp, NH * B + Bp), 128),
            scratch(n, A, G, PR, H, 128),
            scratch(G, H + 2, H, 128),
            scratch(A, B, NH, (PR + 2) * R, 128),
            scratch(A, rows, R, 128),
            scratch(A, H, H, 128),
            scratch(NH * B + G, R, 128),
            scratch(A, B, rows, R, W),
            scratch(n, packet_rows, 128),
            scratch(npair, pair_rows, 128),
            scratch(pair_rows, 128),
            scratch(A, rows, R, 128),
            scratch(A, rows, R, 128),
            scratch(A, H, H, 128),
            scratch(A, H, H, 128),
            scratch(Bp, W),
            scratch(Bp, W),
            scratch(Gp, 128),
            scratch(Gp, 128),
            pltpu.VMEM((group, W, 128), jnp.bfloat16),
            scratch(A, R, 128),
            scratch(A, R, R, 128),
            scratch(A, H * R, 128),
            scratch(R * R, 128),
            dma((A + 1,)), dma((3, A)), dma((2,)), dma((2,)),
            dma((n,)), dma((n,)), dma((n, A)), dma((n, A)),
            dma((2,)), dma((2,)), dma((n,)), dma((n,)), dma((npair,)), dma((npair,)),
        ],
        compiler_params=pltpu.CompilerParams(
            collective_id=0, has_side_effects=True, vmem_limit_bytes=48 * 1024 * 1024
        ),
        name="arc_reverse",
    )(gram_field, cotangent, left_variance, right_flat)
    return out, left, right[:B].reshape(B, R, R)


def solution(mesh):
    in_specs = (
        P("pair", None, "row", None, None),
        P("pair", None, None),
        P(),
        P("pair", "row", None, None, None),
    )
    out_specs = (P("pair", None, "row", None, None), P("pair", None, None), P())
    return jax.shard_map(
        functools.partial(on_device, mesh.shape["row"], mesh.shape["pair"]),
        mesh=mesh, in_specs=in_specs, out_specs=out_specs, check_vma=False,
    )
```

```python
import functools
import math

import jax
import jax.numpy as jnp
from jax import lax
from jax.experimental import pallas as pl
from jax.experimental.pallas import tpu as pltpu
from jax.sharding import PartitionSpec as P

ARCSIN_EVEN = (2.61397078, -1.36807576, 0.342139678, -0.0179491288)
ARCSIN_ROOT = (-1.61397053, 0.727749535, -0.104947558)


def divided(x, k):
    return x >> (k.bit_length() - 1) if k & (k - 1) == 0 else lax.div(x, k)


def left_over(x, k):
    return x & (k - 1) if k & (k - 1) == 0 else lax.rem(x, k)


def lane_of(shape):
    return lax.broadcasted_iota(jnp.int32, shape, len(shape) - 1)


def sub_of(shape):
    return lax.broadcasted_iota(jnp.int32, shape, len(shape) - 2)


def pool_matrix(length, group, t):
    half = length // 2
    shape = (length * length, group * half * half)
    row = sub_of(shape)
    lane = lane_of(shape)
    row_k, row_l = divided(row, length), left_over(row, length)
    lane_t, place = divided(lane, half * half), left_over(lane, half * half)
    same = (
        (lane_t == t)
        & (divided(row_k, 2) == divided(place, half))
        & (divided(row_l, 2) == left_over(place, half))
    )
    return jnp.where(same, 1.0, 0.0).astype(jnp.bfloat16)


def split_dot(x, matrix, dims=((1,), (0,)), terms=2):
    total = None
    for _ in range(terms):
        piece = x.astype(jnp.bfloat16)
        y = lax.dot_general(piece, matrix, (dims, ((), ())), preferred_element_type=jnp.float32)
        total = y if total is None else total + y
        x = x - piece.astype(jnp.float32)
    return total


def arc_parts(rho):
    square = rho * rho
    rest = 1.0 - square
    sine = rest * lax.rsqrt(rest)
    even = ARCSIN_EVEN[3]
    for c in ARCSIN_EVEN[2::-1]:
        even = even * square + c
    root = ARCSIN_ROOT[2]
    for c in ARCSIN_ROOT[1::-1]:
        root = root * square + c
    angle = (0.5 * math.pi) + rho * (even + sine * root)
    return sine, angle


def roll(x, shift, axis):
    return pltpu.roll(x, shift % x.shape[axis], axis)


def lane_masks(shape, side, chunks):
    lane = lane_of(shape)
    sub = sub_of(shape)
    col = left_over(lane, side)
    if chunks > 1:
        k_up, k_down = lane < 128 - side, lane >= side
    else:
        k = left_over(divided(lane, side), side)
        k_up, k_down = k + 1 < side, k >= 1
    l_up, l_down = col + 1 < side, col >= 1
    return k_up, k_down, l_up, l_down, l_up & (sub + 1 < shape[0]), l_down & (sub >= 1)


def shift_k_up(chunks, side, mask):
    rolled = [roll(c, -side, 1) for c in chunks] + [0.0]
    return [jnp.where(mask, rolled[h], rolled[h + 1]) for h in range(len(chunks))]


def shift_k_down(chunks, side, mask):
    rolled = [0.0] + [roll(c, side, 1) for c in chunks]
    return [jnp.where(mask, rolled[h + 1], rolled[h]) for h in range(len(chunks))]


def conv_rows(rows, side, masks):
    k_up, k_down, _, _, v_up, v_down = masks
    out = []
    for i in range(1, len(rows) - 1):
        inner = rows[i]
        if rows[i + 1] is not None:
            inner = [x + y for x, y in zip(inner, shift_k_up(rows[i + 1], side, k_up))]
        if rows[i - 1] is not None:
            inner = [x + y for x, y in zip(inner, shift_k_down(rows[i - 1], side, k_down))]
        done = []
        for x in inner:
            up = jnp.where(v_up, roll(roll(x, -1, 0), -1, 1), 0.0)
            down = jnp.where(v_down, roll(roll(x, 1, 0), 1, 1), 0.0)
            done.append(x + up + down)
        out.append(done)
    return out


def conv_flat(chunks, side, masks):
    k_up, k_down, l_up, l_down, _, _ = masks
    ups = shift_k_up(chunks, side, k_up)
    downs = shift_k_down(chunks, side, k_down)
    out = []
    for x, up, down in zip(chunks, ups, downs):
        x = x + up + down
        x = x + jnp.where(l_up, roll(x, -1, 1), 0.0) + jnp.where(l_down, roll(x, 1, 1), 0.0)
        out.append(x * (1.0 / 9.0))
    return out


def conv_columns(columns):
    count, extent = columns.shape[0], columns.shape[1]
    sub = sub_of((extent, 128))
    out = []
    for i in range(count):
        x = columns[i]
        if i > 0:
            x = x + columns[i - 1]
        if i + 1 < count:
            x = x + columns[i + 1]
        up = jnp.where(sub + 1 < extent, roll(x, -1, 0), 0.0)
        down = jnp.where(sub >= 1, roll(x, 1, 0), 0.0)
        out.append((x + up + down) * (1.0 / 9.0))
    return out


def root_pair(x):
    inverse = lax.rsqrt(x)
    return x * inverse, inverse


def rounded(count):
    return -(-count // 8) * 8


def body(
    sizes,
    gram_hbm, cot_hbm, lv_hbm, rv_hbm,
    out_v, left_out, right_out,
    gram, cot, slope, sinem, kp, tmp, pooled, back, fine, wsum, wsum2, racc, packet, pair_all, pair_packet,
    gl_ref, il_ref, gl2_ref, il2_ref, gr_ref, ir_ref, gr2_ref, ir2_ref, mat_ref, lmap, cols, half_cols, ccol,
    lv_ref, rv_ref, right_flat,
    load_sem, halo_send, halo_recv, cot_send, cot_recv, pool_send, pool_recv,
    slope_send, slope_recv, left_send, left_recv, pair_send, pair_recv,
):
    n, npair, A, B, rows, R, group, part = sizes
    H = R // 2
    W = R * R
    NH = W // 128
    G = B // group
    PR = rows // 2
    Bp = rounded(B)
    Gp = rounded(G)
    LR = A * rows
    me = lax.axis_index("row")
    mine = lax.axis_index("pair")
    f32 = jnp.float32

    def chunk(h):
        return slice(h * 128, (h + 1) * 128)

    barrier = pltpu.get_barrier_semaphore()
    for d in range(1, n):
        pl.semaphore_signal(barrier, inc=1, device_id={"row": lax.rem(me + d, n)})
    for d in range(1, npair):
        pl.semaphore_signal(barrier, inc=1, device_id={"pair": lax.rem(mine + d, npair)})

    loads = []
    for a in range(A):
        c = pltpu.make_async_copy(gram_hbm.at[a], gram.at[a, :, pl.ds(1, rows)], load_sem.at[a])
        c.start()
        loads.append(c)
    cot_load = pltpu.make_async_copy(cot_hbm, cot.at[me], load_sem.at[A])
    cot_load.start()
    left_load = pltpu.make_async_copy(lv_hbm, lv_ref, load_sem.at[A + 1])
    left_load.start()
    right_load = pltpu.make_async_copy(rv_hbm, rv_ref, load_sem.at[A + 2])
    right_load.start()

    pl.semaphore_wait(barrier, n - 1 + npair - 1)

    has_low = me > 0
    has_high = me < n - 1
    low = jnp.maximum(me - 1, 0)
    high = jnp.minimum(me + 1, n - 1)

    def halo_up():
        return pltpu.make_async_remote_copy(
            src_ref=gram_hbm.at[:, :, rows - 1], dst_ref=gram.at[:, :, 0],
            send_sem=halo_send.at[0], recv_sem=halo_recv.at[0], device_id={"row": high})

    def halo_down():
        return pltpu.make_async_remote_copy(
            src_ref=gram_hbm.at[:, :, 0], dst_ref=gram.at[:, :, rows + 1],
            send_sem=halo_send.at[1], recv_sem=halo_recv.at[1], device_id={"row": low})

    def slope_up():
        return pltpu.make_async_remote_copy(
            src_ref=slope.at[:, :, rows], dst_ref=slope.at[:, :, 0],
            send_sem=slope_send.at[0], recv_sem=slope_recv.at[0], device_id={"row": high})

    def slope_down():
        return pltpu.make_async_remote_copy(
            src_ref=slope.at[:, :, 1], dst_ref=slope.at[:, :, rows + 1],
            send_sem=slope_send.at[1], recv_sem=slope_recv.at[1], device_id={"row": low})

    def row_copy(ref, sends, recvs, d):
        return pltpu.make_async_remote_copy(
            src_ref=ref.at[me], dst_ref=ref.at[me], send_sem=sends.at[d],
            recv_sem=recvs.at[me], device_id={"row": lax.rem(me + d, n)})

    def row_arrival(ref, sends, recvs, d):
        source = lax.rem(me + d, n)
        return pltpu.make_async_remote_copy(
            src_ref=ref.at[source], dst_ref=ref.at[source], send_sem=sends.at[d],
            recv_sem=recvs.at[source], device_id={"row": source})

    @pl.when(has_high)
    def _():
        halo_up().start()

    @pl.when(has_low)
    def _():
        halo_down().start()

    cot_load.wait()
    for d in range(1, n):
        row_copy(cot, cot_send, cot_recv, d).start()

    zero_row = jnp.zeros((A, B, R, W), f32)

    @pl.when(jnp.logical_not(has_low))
    def _():
        gram[:, :, 0] = zero_row
        slope[:, :, 0] = zero_row

    @pl.when(jnp.logical_not(has_high))
    def _():
        gram[:, :, rows + 1] = zero_row
        slope[:, :, rows + 1] = zero_row

    for t in range(group):
        mat_ref[t] = pool_matrix(R, group, t)
    ones = jnp.ones((128, 128), jnp.bfloat16)
    left_load.wait()
    right_load.wait()
    lmap[...] = jnp.zeros((A, R, 128), f32)
    lmap[:, :, 0:R] = lv_ref[...]
    sub16 = sub_of((R, 128))
    lane16 = lane_of((R, 128))
    band = jnp.abs(sub16 - lane16) <= 1
    for a in range(A):
        v = lmap[a]
        v = v + jnp.where(sub16 + 1 < R, roll(v, -1, 0), 0.0) + jnp.where(sub16 >= 1, roll(v, 1, 0), 0.0)
        lmap[a] = v
    for a in range(A):
        for i in range(R):
            line = jnp.broadcast_to(lmap[a, i : i + 1, :], (R, 128))
            cols[a, i] = jnp.where(band, line, 0.0)
    spread = split_dot(cols[...].reshape(A * R * R, 128), ones, terms=3) * (1.0 / 9.0)
    cols[...] = spread.reshape(A, R, R, 128)
    for a in range(A):
        for c in range(H):
            half_cols[a, c * R : (c + 1) * R] = cols[a, 2 * c] + cols[a, 2 * c + 1]
    for a in range(A):
        even = half_cols[a, pl.ds(0, H * H, stride=2), :]
        odd = half_cols[a, pl.ds(1, H * H, stride=2), :]
        second = conv_columns(((even + odd) * 0.125).reshape(H, H, 128))
        for i in range(H):
            g2, i2 = root_pair(second[i])
            gl2_ref[a, i] = g2
            il2_ref[a, i] = i2 * (1.0 / 9.0)
        g1, i1 = root_pair(cols[a, pl.ds(me * rows, rows)])
        gl_ref[a] = g1
        il_ref[a] = i1 * (1.0 / 9.0)

    flat_masks = lane_masks((Bp, 128), R, NH)
    flat_masks2 = lane_masks((Gp, 128), H, 1)
    wide_lane = lane_of((R, W))
    here = divided(wide_lane, R) == sub_of((R, W))
    choose = jnp.where(
        left_over(sub_of((W, 128)), R) == lane_of((W, 128)), 1.0, 0.0
    ).astype(jnp.bfloat16)
    right_flat[...] = jnp.ones((Bp, W), f32)
    for b in range(B):
        lmap[0] = jnp.zeros((R, 128), f32)
        lmap[0, :, 0:R] = rv_ref[b]
        tiled = split_dot(lmap[0], choose, ((1,), (1,)), terms=3)
        right_flat[b : b + 1, :] = jnp.sum(jnp.where(here, tiled, 0.0), axis=0, keepdims=True)
    first_right = conv_flat([right_flat[:, chunk(h)] for h in range(NH)], R, flat_masks)
    for h in range(NH):
        gr_ref[:, chunk(h)], ir_ref[:, chunk(h)] = root_pair(first_right[h])
    first_flat = jnp.concatenate(first_right, axis=1)
    small = [split_dot(first_flat, mat_ref[t], terms=3) for t in range(group)]
    gr2_ref[...] = jnp.ones((Gp, 128), f32)
    for g in range(G):
        line = None
        for t in range(group):
            b = g * group + t
            y = small[t][b : b + 1, :]
            line = y if line is None else line + y
        gr2_ref[g : g + 1, :] = line * 0.125
    (second_right,) = conv_flat([gr2_ref[...]], H, flat_masks2)
    gr2_ref[...], ir2_ref[...] = root_pair(second_right)

    for c in loads:
        c.wait()

    masks = lane_masks((R, 128), R, NH)

    def forward(a, b, p):
        f = [[gram[a, b, 2 * p + t, :, chunk(h)] for h in range(NH)] for t in range(4)]
        source = conv_rows(f, R, masks)
        for h in range(NH):
            total = None
            for t in range(2):
                i = 2 * p + t
                m = gl_ref[a, i] * gr_ref[b : b + 1, chunk(h)]
                rho = source[t][h] * (il_ref[a, i] * ir_ref[b : b + 1, chunk(h)])
                sine, angle = arc_parts(rho)
                sm = m * sine
                slope[a, b, i + 1, :, chunk(h)] = angle
                sinem[a, b, i, :, chunk(h)] = sm
                term = sm + m * (angle * rho)
                total = term if total is None else total + term
            kp[b, a, p, :, chunk(h)] = total

    interior = list(range(1, PR - 1))
    edges = sorted({0, PR - 1})

    if interior:
        @pl.loop(0, A, unroll=True)
        def _(a):
            for b in range(B):
                for p in interior:
                    forward(a, b, p)

    @pl.when(has_low)
    def _():
        halo_up().wait_recv()

    @pl.when(has_high)
    def _():
        halo_down().wait_recv()

    @pl.loop(0, A, unroll=True)
    def _(a):
        for b in range(B):
            for p in edges:
                forward(a, b, p)

    for g in range(G):
        acc = None
        for t in range(group):
            y = split_dot(kp[g * group + t].reshape(A * PR * R, W), mat_ref[t])
            acc = y if acc is None else acc + y
        tmp[g, 0 : A * PR * R] = acc
    for g in range(G):
        even = tmp[g, pl.ds(0, A * PR * H, stride=2), :]
        odd = tmp[g, pl.ds(1, A * PR * H, stride=2), :]
        pooled[me, g] = ((even + odd) * (1.0 / (32.0 * math.pi))).reshape(A, PR, H, 128)
    for d in range(1, n):
        row_copy(pooled, pool_send, pool_recv, d).start()

    @pl.when(has_high)
    def _():
        slope_up().start()

    @pl.when(has_low)
    def _():
        slope_down().start()

    for d in range(1, n):
        row_arrival(cot, cot_send, cot_recv, d).wait_recv()

    masks2 = lane_masks((H, 128), H, 1)
    racc[...] = jnp.zeros((NH * B + G, R, 128), f32)

    for d in range(1, n):
        row_arrival(pooled, pool_send, pool_recv, d).wait_recv()

    scale = 1.0 / (9.0 * 2.0 * math.pi * 16.0) / (18.0 * math.pi)
    zero = jnp.zeros((H, 128), f32)
    for g in range(G):
        sources = []
        for a in range(A):
            f = [None] + [[pooled[i // PR, g, a, i % PR]] for i in range(H)] + [None]
            sources.append(conv_rows(f, H, masks2))
        cts = []
        right2 = None
        for a in range(A):
            ct = [None]
            for i in range(H):
                m = gl2_ref[a, i] * gr2_ref[g : g + 1, :]
                rho = sources[a][i][0] * (il2_ref[a, i] * ir2_ref[g : g + 1, :])
                sine, angle = arc_parts(rho)
                pieces = []
                for t in range(group):
                    b = g * group + t
                    pieces.append(cot[b // part, a, b % part, i])
                c = jnp.concatenate(pieces, axis=1)
                ct.append([c * angle])
                w = c * (m * sine)
                right2 = w if right2 is None else right2 + w
                wsum2[a, i] = w if g == 0 else wsum2[a, i] + w
            ct.append(None)
            cts.append(ct)
        racc[NH * B + g, 0:H] = right2
        for a in range(A):
            b_rows = conv_rows(cts[a], H, masks2)
            back[a, 0] = zero
            back[a, H + 1] = zero
            for i in range(H):
                back[a, i + 1] = b_rows[i][0] * scale
        x = back[:, pl.ds(me * PR, PR + 2)].reshape(A * (PR + 2) * H, 128)
        for t in range(group):
            y = split_dot(x, mat_ref[t], ((1,), (1,)))
            for h in range(NH):
                fine[g * group + t, h, pl.ds(0, A * (PR + 2) * H, stride=2), :] = y[:, chunk(h)]
                fine[g * group + t, h, pl.ds(1, A * (PR + 2) * H, stride=2), :] = y[:, chunk(h)]

    def fine_row(a, b, h, c):
        first = (a * (PR + 2) + c) * R
        if not isinstance(first, int):
            first = pl.multiple_of(first, 8)
        return fine[b, h, pl.ds(first, R), :]

    @pl.loop(0, A, unroll=True)
    def _(a):
        lsum = [None] * rows
        for b in range(B):
            for h in range(NH):
                total = None
                for p in range(PR):
                    bk = fine_row(a, b, h, p + 1)
                    for t in range(2):
                        i = 2 * p + t
                        w = bk * sinem[a, b, i, :, chunk(h)]
                        total = w if total is None else total + w
                        lsum[i] = w if lsum[i] is None else lsum[i] + w
                racc[h * B + b] = racc[h * B + b] + total
        for i in range(rows):
            wsum[a, i] = lsum[i]

    diagonal = (sub16 == lane16)[None]
    sums = split_dot(wsum[...].reshape(LR * R, 128), ones).reshape(LR, R, 128)
    inverse = il_ref[...].reshape(LR, R, 128)
    sums = sums * (inverse * inverse * (4.5 * 81.0))
    packet[me, 0:LR, :] = jnp.sum(jnp.where(diagonal, sums, 0.0), axis=1)
    right_sums = jnp.sum(racc[...], axis=1)
    packet[me, LR : LR + NH * B, :] = right_sums[0 : NH * B]
    for d in range(1, n):
        row_copy(packet, left_send, left_recv, d).start()

    def final(a, b, chosen):
        cache = {}

        def product(i):
            if i not in cache:
                c = (i + 1) // 2
                cache[i] = [
                    fine_row(a, b, h, c) * slope[a, b, i, :, chunk(h)] for h in range(NH)
                ]
            return cache[i]

        for i in chosen:
            (value,) = conv_rows([product(i - 1), product(i), product(i + 1)], R, masks)
            for h in range(NH):
                out_v[a, b, i - 1, :, chunk(h)] = value[h]

    if rows > 2:
        @pl.loop(0, A, unroll=True)
        def _(a):
            for b in range(B):
                final(a, b, range(2, rows))

    for d in range(1, n):
        row_arrival(packet, left_send, left_recv, d).wait_recv()
    right = packet[0, LR : LR + NH * B, :]
    for r in range(1, n):
        right = right + packet[r, LR : LR + NH * B, :]
    pair_packet[...] = jnp.zeros(pair_packet.shape, f32)
    pair_packet[0 : NH * B, :] = right
    pair_packet[NH * B : NH * B + G, :] = right_sums[NH * B : NH * B + G]
    pair_all[mine] = pair_packet[...]

    def pair_copy(d):
        return pltpu.make_async_remote_copy(
            src_ref=pair_packet, dst_ref=pair_all.at[mine], send_sem=pair_send.at[d],
            recv_sem=pair_recv.at[mine], device_id={"pair": lax.rem(mine + d, npair)})

    def pair_arrival(d):
        source = lax.rem(mine + d, npair)
        return pltpu.make_async_remote_copy(
            src_ref=pair_packet, dst_ref=pair_all.at[source], send_sem=pair_send.at[d],
            recv_sem=pair_recv.at[source], device_id={"pair": source})

    for d in range(1, npair):
        pair_copy(d).start()

    @pl.when(has_low)
    def _():
        slope_up().wait_recv()

    @pl.when(has_high)
    def _():
        slope_down().wait_recv()

    @pl.loop(0, A, unroll=True)
    def _(a):
        for b in range(B):
            final(a, b, sorted({1, rows}))

    inverse2 = il2_ref[...].reshape(A * H, H, 128)
    sums2 = split_dot(wsum2[...].reshape(A * H * H, 128), ones).reshape(A * H, H, 128)
    sums2 = sums2 * (inverse2 * inverse2 * (81.0 / (4.0 * math.pi * 8.0)))
    for a in range(A):
        mixed = conv_columns(sums2[a * H : (a + 1) * H])
        for c in range(H):
            for t in range(2):
                ccol[pl.ds((2 * c + t) * R, H, stride=2), :] = mixed[c]
                ccol[pl.ds((2 * c + t) * R + 1, H, stride=2), :] = mixed[c]
        coarse = jnp.sum(jnp.where(diagonal, ccol[...].reshape(R, R, 128), 0.0), axis=1)
        local = jnp.concatenate([packet[r, a * rows : (a + 1) * rows, :] for r in range(n)], axis=0)
        v = coarse + local
        v = v + jnp.where(sub16 + 1 < R, roll(v, -1, 0), 0.0) + jnp.where(sub16 >= 1, roll(v, 1, 0), 0.0)
        v = (v + roll(v, 1, 1) + roll(v, -1, 1)) * (1.0 / 9.0)
        left_out[a] = v[:, 0:R]

    for d in range(1, npair):
        pair_arrival(d).wait_recv()
    total = pair_all[0]
    for r in range(1, npair):
        total = total + pair_all[r]
    pair_packet_rows = pair_packet.shape[0]
    tmp[0, 0:pair_packet_rows, :] = total
    tmp[0, pair_packet_rows : pair_packet_rows + Gp, :] = jnp.zeros((Gp, 128), f32)
    coarse = tmp[0, NH * B : NH * B + Gp, :]
    (coarse,) = conv_flat([coarse * (ir2_ref[...] * ir2_ref[...] * (1.0 / (4.0 * math.pi * 8.0)))], H, flat_masks2)
    wide = [split_dot(coarse, mat_ref[t], ((1,), (1,)), terms=3) for t in range(group)]
    right_flat[...] = jnp.zeros((Bp, W), f32)
    for b in range(B):
        right_flat[b : b + 1, :] = wide[b % group][b // group : b // group + 1, :]
    pieces = []
    for h in range(NH):
        scale = ir_ref[:, chunk(h)]
        pieces.append(right_flat[:, chunk(h)] + tmp[0, h * B : h * B + Bp, :] * (scale * scale * 4.5))
    pieces = conv_flat(pieces, R, flat_masks)
    for h in range(NH):
        right_flat[:, chunk(h)] = pieces[h]
    for b in range(B):
        line = jnp.where(here, jnp.broadcast_to(right_flat[b : b + 1, :], (R, W)), 0.0)
        right_out[b] = split_dot(line, choose, terms=3)[:, 0:R]

    @pl.when(has_high)
    def _():
        halo_up().wait_send()
        slope_up().wait_send()

    @pl.when(has_low)
    def _():
        halo_down().wait_send()
        slope_down().wait_send()

    for d in range(1, n):
        row_copy(cot, cot_send, cot_recv, d).wait_send()
        row_copy(packet, left_send, left_recv, d).wait_send()
        row_copy(pooled, pool_send, pool_recv, d).wait_send()
    for d in range(1, npair):
        pair_copy(d).wait_send()


def store_body(a_ref, b_ref, c_ref, a_out, b_out, c_out, sems):
    copies = [
        pltpu.make_async_copy(source, target, sems.at[i])
        for i, (source, target) in enumerate(((a_ref, a_out), (b_ref, b_out), (c_ref, c_out)))
    ]
    for c in copies:
        c.start()
    for c in copies:
        c.wait()


def on_device(n, npair, gram_field, left_variance, right_variance, cotangent):
    A, B, rows, R, W = gram_field.shape
    part = cotangent.shape[1]
    H = R // 2
    NH = W // 128
    width = H * H
    group = 128 // width
    G = B // group
    PR = rows // 2
    Bp, Gp = rounded(B), rounded(G)
    f32 = jnp.float32

    pair_rows = rounded(NH * B + G)
    packet_rows = rounded(A * rows + NH * B)
    sizes = (n, npair, A, B, rows, R, group, part)
    vmem = pl.BlockSpec(memory_space=pltpu.VMEM)
    hbm = pl.BlockSpec(memory_space=pltpu.HBM)
    dma = pltpu.SemaphoreType.DMA

    def scratch(*shape):
        return pltpu.VMEM(shape, f32)

    shapes = tuple(
        jax.ShapeDtypeStruct(x.shape, f32) for x in (gram_field, left_variance, right_variance)
    )
    results = pl.pallas_call(
        functools.partial(body, sizes),
        out_shape=shapes,
        in_specs=[hbm] * 4,
        out_specs=(vmem,) * 3,
        scratch_shapes=[
            scratch(A, B, rows + 2, R, W),
            scratch(n, A, part, H, H, width),
            scratch(A, B, rows + 2, R, W),
            scratch(A, B, rows, R, W),
            scratch(B, A, PR, R, W),
            scratch(G, max(A * PR * R, pair_rows + Gp, NH * B + Bp), 128),
            scratch(n, G, A, PR, H, 128),
            scratch(A, H + 2, H, 128),
            scratch(B, NH, A * (PR + 2) * R, 128),
            scratch(A, rows, R, 128),
            scratch(A, H, H, 128),
            scratch(NH * B + G, R, 128),
            scratch(n, packet_rows, 128),
            scratch(npair, pair_rows, 128),
            scratch(pair_rows, 128),
            scratch(A, rows, R, 128),
            scratch(A, rows, R, 128),
            scratch(A, H, H, 128),
            scratch(A, H, H, 128),
            scratch(Bp, W),
            scratch(Bp, W),
            scratch(Gp, 128),
            scratch(Gp, 128),
            pltpu.VMEM((group, W, 128), jnp.bfloat16),
            scratch(A, R, 128),
            scratch(A, R, R, 128),
            scratch(A, H * R, 128),
            scratch(R * R, 128),
            scratch(A, R, R),
            scratch(B, R, R),
            scratch(Bp, W),
            dma((A + 3,)), dma((2,)), dma((2,)),
            dma((n,)), dma((n,)), dma((n,)), dma((n,)),
            dma((2,)), dma((2,)), dma((n,)), dma((n,)), dma((npair,)), dma((npair,)),
        ],
        compiler_params=pltpu.CompilerParams(
            collective_id=0, has_side_effects=True, vmem_limit_bytes=48 * 1024 * 1024
        ),
        name="arc_reverse",
    )(gram_field, cotangent, left_variance, right_variance)
    return pl.pallas_call(
        store_body,
        out_shape=shapes,
        in_specs=[vmem] * 3,
        out_specs=(hbm,) * 3,
        scratch_shapes=[dma((3,))],
        name="store_results",
    )(*results)


def solution(mesh):
    in_specs = (
        P("pair", None, "row", None, None),
        P("pair", None, None),
        P(),
        P("pair", "row", None, None, None),
    )
    out_specs = (P("pair", None, "row", None, None), P("pair", None, None), P())
    return jax.shard_map(
        functools.partial(on_device, mesh.shape["row"], mesh.shape["pair"]),
        mesh=mesh, in_specs=in_specs, out_specs=out_specs, check_vma=False,
    )
```

```python
import functools
import math

import jax
import jax.numpy as jnp
from jax import lax
from jax.experimental import pallas as pl
from jax.experimental.pallas import tpu as pltpu
from jax.sharding import PartitionSpec as P

ARCSIN_EVEN = (2.61397078, -1.36807576, 0.342139678, -0.0179491288)
ARCSIN_ROOT = (-1.61397053, 0.727749535, -0.104947558)


def divided(x, k):
    return x >> (k.bit_length() - 1) if k & (k - 1) == 0 else lax.div(x, k)


def left_over(x, k):
    return x & (k - 1) if k & (k - 1) == 0 else lax.rem(x, k)


def lane_of(shape):
    return lax.broadcasted_iota(jnp.int32, shape, len(shape) - 1)


def sub_of(shape):
    return lax.broadcasted_iota(jnp.int32, shape, len(shape) - 2)


def pool_matrix(length, group, t):
    half = length // 2
    shape = (length * length, group * half * half)
    row = sub_of(shape)
    lane = lane_of(shape)
    row_k, row_l = divided(row, length), left_over(row, length)
    lane_t, place = divided(lane, half * half), left_over(lane, half * half)
    same = (
        (lane_t == t)
        & (divided(row_k, 2) == divided(place, half))
        & (divided(row_l, 2) == left_over(place, half))
    )
    return jnp.where(same, 1.0, 0.0).astype(jnp.bfloat16)


def split_dot(x, matrix, dims=((1,), (0,)), terms=2):
    total = None
    for _ in range(terms):
        piece = x.astype(jnp.bfloat16)
        y = lax.dot_general(piece, matrix, (dims, ((), ())), preferred_element_type=jnp.float32)
        total = y if total is None else total + y
        x = x - piece.astype(jnp.float32)
    return total


def arc_parts(rho):
    square = rho * rho
    rest = 1.0 - square
    sine = rest * lax.rsqrt(rest)
    even = ARCSIN_EVEN[3]
    for c in ARCSIN_EVEN[2::-1]:
        even = even * square + c
    root = ARCSIN_ROOT[2]
    for c in ARCSIN_ROOT[1::-1]:
        root = root * square + c
    angle = (0.5 * math.pi) + rho * (even + sine * root)
    return sine, angle


def roll(x, shift, axis):
    return pltpu.roll(x, shift % x.shape[axis], axis)


def lane_masks(shape, side, chunks):
    lane = lane_of(shape)
    sub = sub_of(shape)
    col = left_over(lane, side)
    if chunks > 1:
        k_up, k_down = lane < 128 - side, lane >= side
    else:
        k = left_over(divided(lane, side), side)
        k_up, k_down = k + 1 < side, k >= 1
    l_up, l_down = col + 1 < side, col >= 1
    return k_up, k_down, l_up, l_down, l_up & (sub + 1 < shape[0]), l_down & (sub >= 1)


def shift_k_up(chunks, side, mask):
    rolled = [roll(c, -side, 1) for c in chunks] + [0.0]
    return [jnp.where(mask, rolled[h], rolled[h + 1]) for h in range(len(chunks))]


def shift_k_down(chunks, side, mask):
    rolled = [0.0] + [roll(c, side, 1) for c in chunks]
    return [jnp.where(mask, rolled[h + 1], rolled[h]) for h in range(len(chunks))]


def conv_rows(rows, side, masks):
    k_up, k_down, _, _, v_up, v_down = masks
    out = []
    for i in range(1, len(rows) - 1):
        inner = rows[i]
        if rows[i + 1] is not None:
            inner = [x + y for x, y in zip(inner, shift_k_up(rows[i + 1], side, k_up))]
        if rows[i - 1] is not None:
            inner = [x + y for x, y in zip(inner, shift_k_down(rows[i - 1], side, k_down))]
        done = []
        for x in inner:
            up = jnp.where(v_up, roll(roll(x, -1, 0), -1, 1), 0.0)
            down = jnp.where(v_down, roll(roll(x, 1, 0), 1, 1), 0.0)
            done.append(x + up + down)
        out.append(done)
    return out


def conv_flat(chunks, side, masks):
    k_up, k_down, l_up, l_down, _, _ = masks
    ups = shift_k_up(chunks, side, k_up)
    downs = shift_k_down(chunks, side, k_down)
    out = []
    for x, up, down in zip(chunks, ups, downs):
        x = x + up + down
        x = x + jnp.where(l_up, roll(x, -1, 1), 0.0) + jnp.where(l_down, roll(x, 1, 1), 0.0)
        out.append(x * (1.0 / 9.0))
    return out


def conv_columns(columns):
    count, extent = columns.shape[0], columns.shape[1]
    sub = sub_of((extent, 128))
    out = []
    for i in range(count):
        x = columns[i]
        if i > 0:
            x = x + columns[i - 1]
        if i + 1 < count:
            x = x + columns[i + 1]
        up = jnp.where(sub + 1 < extent, roll(x, -1, 0), 0.0)
        down = jnp.where(sub >= 1, roll(x, 1, 0), 0.0)
        out.append((x + up + down) * (1.0 / 9.0))
    return out


def root_pair(x):
    inverse = lax.rsqrt(x)
    return x * inverse, inverse


def rounded(count):
    return -(-count // 8) * 8


def body(
    sizes,
    gram_hbm, cot_hbm, lv_hbm, rv_hbm,
    out_hbm, left_out, right_out,
    gram, cot, slope, sinem, kp, tmp, pooled, back, fine, wsum, wsum2, racc, out_v, packet, pair_all, pair_packet,
    gl_ref, il_ref, gl2_ref, il2_ref, gr_ref, ir_ref, gr2_ref, ir2_ref, mat_ref, lmap, cols, half_cols, ccol,
    lv_ref, rv_ref, right_flat,
    load_sem, out_sem, halo_send, halo_recv, cot_send, cot_recv, pool_send, pool_recv,
    slope_send, slope_recv, left_send, left_recv, pair_send, pair_recv,
):
    n, npair, A, B, rows, R, group, part = sizes
    H = R // 2
    W = R * R
    NH = W // 128
    G = B // group
    PR = rows // 2
    Bp = rounded(B)
    Gp = rounded(G)
    LR = A * rows
    me = lax.axis_index("row")
    mine = lax.axis_index("pair")
    f32 = jnp.float32

    def chunk(h):
        return slice(h * 128, (h + 1) * 128)

    barrier = pltpu.get_barrier_semaphore()
    for d in range(1, n):
        pl.semaphore_signal(barrier, inc=1, device_id={"row": lax.rem(me + d, n)})

    @pl.loop(1, npair)
    def _(d):
        pl.semaphore_signal(barrier, inc=1, device_id={"pair": lax.rem(mine + d, npair)})

    loads = []
    for a in range(A):
        c = pltpu.make_async_copy(gram_hbm.at[a], gram.at[a, :, pl.ds(1, rows)], load_sem.at[a])
        c.start()
        loads.append(c)
    cot_load = pltpu.make_async_copy(cot_hbm, cot.at[me], load_sem.at[A])
    cot_load.start()
    left_load = pltpu.make_async_copy(lv_hbm, lv_ref, load_sem.at[A + 1])
    left_load.start()
    right_load = pltpu.make_async_copy(rv_hbm, rv_ref, load_sem.at[A + 2])
    right_load.start()

    pl.semaphore_wait(barrier, n - 1 + npair - 1)

    has_low = me > 0
    has_high = me < n - 1
    low = jnp.maximum(me - 1, 0)
    high = jnp.minimum(me + 1, n - 1)

    def halo_up():
        return pltpu.make_async_remote_copy(
            src_ref=gram_hbm.at[:, :, rows - 1], dst_ref=gram.at[:, :, 0],
            send_sem=halo_send.at[0], recv_sem=halo_recv.at[0], device_id={"row": high})

    def halo_down():
        return pltpu.make_async_remote_copy(
            src_ref=gram_hbm.at[:, :, 0], dst_ref=gram.at[:, :, rows + 1],
            send_sem=halo_send.at[1], recv_sem=halo_recv.at[1], device_id={"row": low})

    def slope_up():
        return pltpu.make_async_remote_copy(
            src_ref=slope.at[:, :, rows], dst_ref=slope.at[:, :, 0],
            send_sem=slope_send.at[0], recv_sem=slope_recv.at[0], device_id={"row": high})

    def slope_down():
        return pltpu.make_async_remote_copy(
            src_ref=slope.at[:, :, 1], dst_ref=slope.at[:, :, rows + 1],
            send_sem=slope_send.at[1], recv_sem=slope_recv.at[1], device_id={"row": low})

    def row_copy(ref, sends, recvs, d):
        return pltpu.make_async_remote_copy(
            src_ref=ref.at[me], dst_ref=ref.at[me], send_sem=sends.at[d],
            recv_sem=recvs.at[me], device_id={"row": lax.rem(me + d, n)})

    def row_arrival(ref, sends, recvs, d):
        source = lax.rem(me + d, n)
        return pltpu.make_async_remote_copy(
            src_ref=ref.at[source], dst_ref=ref.at[source], send_sem=sends.at[d],
            recv_sem=recvs.at[source], device_id={"row": source})

    @pl.when(has_high)
    def _():
        halo_up().start()

    @pl.when(has_low)
    def _():
        halo_down().start()

    cot_load.wait()
    for d in range(1, n):
        row_copy(cot, cot_send, cot_recv, d).start()

    zero_row = jnp.zeros((A, B, R, W), f32)

    @pl.when(jnp.logical_not(has_low))
    def _():
        gram[:, :, 0] = zero_row
        slope[:, :, 0] = zero_row

    @pl.when(jnp.logical_not(has_high))
    def _():
        gram[:, :, rows + 1] = zero_row
        slope[:, :, rows + 1] = zero_row

    for t in range(group):
        mat_ref[t] = pool_matrix(R, group, t)
    ones = jnp.ones((128, 128), jnp.bfloat16)
    left_load.wait()
    right_load.wait()
    lmap[...] = jnp.zeros((A, R, 128), f32)
    lmap[:, :, 0:R] = lv_ref[...]
    sub16 = sub_of((R, 128))
    lane16 = lane_of((R, 128))
    band = jnp.abs(sub16 - lane16) <= 1

    @pl.loop(0, A)
    def _(a):
        v = lmap[a]
        v = v + jnp.where(sub16 + 1 < R, roll(v, -1, 0), 0.0) + jnp.where(sub16 >= 1, roll(v, 1, 0), 0.0)
        lines = []
        for i in range(R):
            lines.append(jnp.where(band, jnp.broadcast_to(v[i : i + 1, :], (R, 128)), 0.0))
        spread = split_dot(jnp.concatenate(lines, axis=0), ones, terms=3) * (1.0 / 9.0)
        cols[...] = spread.reshape(R, R, 128)
        for c in range(H):
            half_cols[c * R : (c + 1) * R] = cols[2 * c] + cols[2 * c + 1]
        even = half_cols[pl.ds(0, H * H, stride=2), :]
        odd = half_cols[pl.ds(1, H * H, stride=2), :]
        second = conv_columns(((even + odd) * 0.125).reshape(H, H, 128))
        for i in range(H):
            g2, i2 = root_pair(second[i])
            gl2_ref[a, i] = g2
            il2_ref[a, i] = i2 * (1.0 / 9.0)
        g1, i1 = root_pair(cols[pl.ds(me * rows, rows)])
        gl_ref[a] = g1
        il_ref[a] = i1 * (1.0 / 9.0)

    flat_masks = lane_masks((Bp, 128), R, NH)
    flat_masks2 = lane_masks((Gp, 128), H, 1)
    wide_lane = lane_of((R, W))
    here = divided(wide_lane, R) == sub_of((R, W))
    choose = jnp.where(
        left_over(sub_of((W, 128)), R) == lane_of((W, 128)), 1.0, 0.0
    ).astype(jnp.bfloat16)
    right_flat[...] = jnp.ones((Bp, W), f32)
    for b in range(B):
        lmap[0] = jnp.zeros((R, 128), f32)
        lmap[0, :, 0:R] = rv_ref[b]
        tiled = split_dot(lmap[0], choose, ((1,), (1,)), terms=3)
        right_flat[b : b + 1, :] = jnp.sum(jnp.where(here, tiled, 0.0), axis=0, keepdims=True)
    first_right = conv_flat([right_flat[:, chunk(h)] for h in range(NH)], R, flat_masks)
    for h in range(NH):
        gr_ref[:, chunk(h)], ir_ref[:, chunk(h)] = root_pair(first_right[h])
    first_flat = jnp.concatenate(first_right, axis=1)
    small = [split_dot(first_flat, mat_ref[t], terms=3) for t in range(group)]
    gr2_ref[...] = jnp.ones((Gp, 128), f32)
    for g in range(G):
        line = None
        for t in range(group):
            b = g * group + t
            y = small[t][b : b + 1, :]
            line = y if line is None else line + y
        gr2_ref[g : g + 1, :] = line * 0.125
    (second_right,) = conv_flat([gr2_ref[...]], H, flat_masks2)
    gr2_ref[...], ir2_ref[...] = root_pair(second_right)

    for c in loads:
        c.wait()

    masks = lane_masks((R, 128), R, NH)

    def forward(a, b, p):
        f = [[gram[a, b, 2 * p + t, :, chunk(h)] for h in range(NH)] for t in range(4)]
        source = conv_rows(f, R, masks)
        for h in range(NH):
            total = None
            for t in range(2):
                i = 2 * p + t
                m = gl_ref[a, i] * gr_ref[b : b + 1, chunk(h)]
                rho = source[t][h] * (il_ref[a, i] * ir_ref[b : b + 1, chunk(h)])
                sine, angle = arc_parts(rho)
                sm = m * sine
                slope[a, b, i + 1, :, chunk(h)] = angle
                sinem[a, b, i, :, chunk(h)] = sm
                term = sm + m * (angle * rho)
                total = term if total is None else total + term
            kp[b, a, p, :, chunk(h)] = total

    early = max(PR - 2, 0)

    def ordered(step):
        q = divided(step, A)
        p = jnp.where(q < early, q + 1, jnp.where(q == PR - 2, 0, PR - 1))
        return left_over(step, A), p

    @pl.loop(0, A * PR)
    def _(step):
        @pl.when(step == early * A)
        def _():
            @pl.when(has_low)
            def _():
                halo_up().wait_recv()

            @pl.when(has_high)
            def _():
                halo_down().wait_recv()

        a, p = ordered(step)
        for b in range(B):
            forward(a, b, p)

    for g in range(G):
        acc = None
        for t in range(group):
            y = split_dot(kp[g * group + t].reshape(A * PR * R, W), mat_ref[t])
            acc = y if acc is None else acc + y
        tmp[g, 0 : A * PR * R] = acc
    for g in range(G):
        even = tmp[g, pl.ds(0, A * PR * H, stride=2), :]
        odd = tmp[g, pl.ds(1, A * PR * H, stride=2), :]
        pooled[me, g] = ((even + odd) * (1.0 / (32.0 * math.pi))).reshape(A, PR, H, 128)
    for d in range(1, n):
        row_copy(pooled, pool_send, pool_recv, d).start()

    @pl.when(has_high)
    def _():
        slope_up().start()

    @pl.when(has_low)
    def _():
        slope_down().start()

    for d in range(1, n):
        row_arrival(cot, cot_send, cot_recv, d).wait_recv()

    masks2 = lane_masks((H, 128), H, 1)
    racc[...] = jnp.zeros((NH * B + G, R, 128), f32)

    for d in range(1, n):
        row_arrival(pooled, pool_send, pool_recv, d).wait_recv()

    scale = 1.0 / (9.0 * 2.0 * math.pi * 16.0) / (18.0 * math.pi)
    zero = jnp.zeros((H, 128), f32)
    for g in range(G):
        sources = []
        for a in range(A):
            f = [None] + [[pooled[i // PR, g, a, i % PR]] for i in range(H)] + [None]
            sources.append(conv_rows(f, H, masks2))
        cts = []
        right2 = None
        for a in range(A):
            ct = [None]
            for i in range(H):
                m = gl2_ref[a, i] * gr2_ref[g : g + 1, :]
                rho = sources[a][i][0] * (il2_ref[a, i] * ir2_ref[g : g + 1, :])
                sine, angle = arc_parts(rho)
                pieces = []
                for t in range(group):
                    b = g * group + t
                    pieces.append(cot[b // part, a, b % part, i])
                c = jnp.concatenate(pieces, axis=1)
                ct.append([c * angle])
                w = c * (m * sine)
                right2 = w if right2 is None else right2 + w
                wsum2[a, i] = w if g == 0 else wsum2[a, i] + w
            ct.append(None)
            cts.append(ct)
        racc[NH * B + g, 0:H] = right2
        for a in range(A):
            b_rows = conv_rows(cts[a], H, masks2)
            back[a, 0] = zero
            back[a, H + 1] = zero
            for i in range(H):
                back[a, i + 1] = b_rows[i][0] * scale
        x = back[:, pl.ds(me * PR, PR + 2)].reshape(A * (PR + 2) * H, 128)
        for t in range(group):
            y = split_dot(x, mat_ref[t], ((1,), (1,)))
            for h in range(NH):
                fine[g * group + t, h, pl.ds(0, A * (PR + 2) * H, stride=2), :] = y[:, chunk(h)]
                fine[g * group + t, h, pl.ds(1, A * (PR + 2) * H, stride=2), :] = y[:, chunk(h)]

    def fine_row(a, b, h, c):
        first = (a * (PR + 2) + c) * R
        if not isinstance(first, int):
            first = pl.multiple_of(first, 8)
        return fine[b, h, pl.ds(first, R), :]

    @pl.loop(0, A)
    def _(a):
        lsum = [None] * rows
        for b in range(B):
            for h in range(NH):
                total = None
                for p in range(PR):
                    bk = fine_row(a, b, h, p + 1)
                    for t in range(2):
                        i = 2 * p + t
                        w = bk * sinem[a, b, i, :, chunk(h)]
                        total = w if total is None else total + w
                        lsum[i] = w if lsum[i] is None else lsum[i] + w
                racc[h * B + b] = racc[h * B + b] + total
        for i in range(rows):
            wsum[a, i] = lsum[i]

    diagonal = (sub16 == lane16)[None]
    sums = split_dot(wsum[...].reshape(LR * R, 128), ones).reshape(LR, R, 128)
    inverse = il_ref[...].reshape(LR, R, 128)
    sums = sums * (inverse * inverse * (4.5 * 81.0))
    packet[me, 0:LR, :] = jnp.sum(jnp.where(diagonal, sums, 0.0), axis=1)
    right_sums = jnp.sum(racc[...], axis=1)
    packet[me, LR : LR + NH * B, :] = right_sums[0 : NH * B]
    for d in range(1, n):
        row_copy(packet, left_send, left_recv, d).start()

    def final(a, b, p):
        f = [
            [fine_row(a, b, h, p + (t + 1) // 2) * slope[a, b, 2 * p + t, :, chunk(h)] for h in range(NH)]
            for t in range(4)
        ]
        value = conv_rows(f, R, masks)
        for t in range(2):
            for h in range(NH):
                out_v[a, b, 2 * p + t, :, chunk(h)] = value[t][h]

    def store(a, p):
        two = pl.ds(2 * p, 2)
        return pltpu.make_async_copy(out_v.at[a, :, two], out_hbm.at[a, :, two], out_sem.at[a, p])

    def pair_copy(d):
        return pltpu.make_async_remote_copy(
            src_ref=pair_packet, dst_ref=pair_all.at[mine], send_sem=pair_send.at[d],
            recv_sem=pair_recv.at[mine], device_id={"pair": lax.rem(mine + d, npair)})

    def pair_arrival(d):
        source = lax.rem(mine + d, npair)
        return pltpu.make_async_remote_copy(
            src_ref=pair_packet, dst_ref=pair_all.at[source], send_sem=pair_send.at[d],
            recv_sem=pair_recv.at[source], device_id={"pair": source})

    pair_packet[...] = jnp.zeros(pair_packet.shape, f32)
    pair_packet[NH * B : NH * B + G, :] = right_sums[NH * B : NH * B + G]

    @pl.loop(0, A * PR)
    def _(step):
        @pl.when(step == early * A)
        def _():
            for d in range(1, n):
                row_arrival(packet, left_send, left_recv, d).wait_recv()
            right = packet[0, LR : LR + NH * B, :]
            for r in range(1, n):
                right = right + packet[r, LR : LR + NH * B, :]
            pair_packet[0 : NH * B, :] = right
            pair_all[mine] = pair_packet[...]

            @pl.loop(1, npair)
            def _(d):
                pair_copy(d).start()

            @pl.when(has_low)
            def _():
                slope_up().wait_recv()

            @pl.when(has_high)
            def _():
                slope_down().wait_recv()

        a, p = ordered(step)
        for b in range(B):
            final(a, b, p)
        store(a, p).start()

    inverse2 = il2_ref[...].reshape(A * H, H, 128)
    sums2 = split_dot(wsum2[...].reshape(A * H * H, 128), ones).reshape(A * H, H, 128)
    sums2 = sums2 * (inverse2 * inverse2 * (81.0 / (4.0 * math.pi * 8.0)))
    wsum2[...] = sums2.reshape(A, H, H, 128)

    @pl.loop(0, A)
    def _(a):
        mixed = conv_columns(wsum2[a])
        for c in range(H):
            for t in range(2):
                ccol[pl.ds((2 * c + t) * R, H, stride=2), :] = mixed[c]
                ccol[pl.ds((2 * c + t) * R + 1, H, stride=2), :] = mixed[c]
        coarse = jnp.sum(jnp.where(diagonal, ccol[...].reshape(R, R, 128), 0.0), axis=1)
        local = jnp.concatenate([packet[r, pl.ds(a * rows, rows), :] for r in range(n)], axis=0)
        v = coarse + local
        v = v + jnp.where(sub16 + 1 < R, roll(v, -1, 0), 0.0) + jnp.where(sub16 >= 1, roll(v, 1, 0), 0.0)
        v = (v + roll(v, 1, 1) + roll(v, -1, 1)) * (1.0 / 9.0)
        left_out[a] = v[:, 0:R]

    @pl.loop(1, npair)
    def _(d):
        pair_arrival(d).wait_recv()
    total = pair_all[0]
    for r in range(1, npair):
        total = total + pair_all[r]
    pair_packet_rows = pair_packet.shape[0]
    tmp[0, 0:pair_packet_rows, :] = total
    tmp[0, pair_packet_rows : pair_packet_rows + Gp, :] = jnp.zeros((Gp, 128), f32)
    coarse = tmp[0, NH * B : NH * B + Gp, :]
    (coarse,) = conv_flat([coarse * (ir2_ref[...] * ir2_ref[...] * (1.0 / (4.0 * math.pi * 8.0)))], H, flat_masks2)
    wide = [split_dot(coarse, mat_ref[t], ((1,), (1,)), terms=3) for t in range(group)]
    right_flat[...] = jnp.zeros((Bp, W), f32)
    for b in range(B):
        right_flat[b : b + 1, :] = wide[b % group][b // group : b // group + 1, :]
    pieces = []
    for h in range(NH):
        scale = ir_ref[:, chunk(h)]
        pieces.append(right_flat[:, chunk(h)] + tmp[0, h * B : h * B + Bp, :] * (scale * scale * 4.5))
    pieces = conv_flat(pieces, R, flat_masks)
    for h in range(NH):
        right_flat[:, chunk(h)] = pieces[h]
    for b in range(B):
        line = jnp.where(here, jnp.broadcast_to(right_flat[b : b + 1, :], (R, W)), 0.0)
        right_out[b] = split_dot(line, choose, terms=3)[:, 0:R]

    @pl.loop(0, A * PR)
    def _(step):
        a, p = ordered(step)
        store(a, p).wait()

    @pl.when(has_high)
    def _():
        halo_up().wait_send()
        slope_up().wait_send()

    @pl.when(has_low)
    def _():
        halo_down().wait_send()
        slope_down().wait_send()

    for d in range(1, n):
        row_copy(cot, cot_send, cot_recv, d).wait_send()
        row_copy(packet, left_send, left_recv, d).wait_send()
        row_copy(pooled, pool_send, pool_recv, d).wait_send()

    @pl.loop(1, npair)
    def _(d):
        pair_copy(d).wait_send()


def on_device(n, npair, gram_field, left_variance, right_variance, cotangent):
    A, B, rows, R, W = gram_field.shape
    part = cotangent.shape[1]
    H = R // 2
    NH = W // 128
    width = H * H
    group = 128 // width
    G = B // group
    PR = rows // 2
    Bp, Gp = rounded(B), rounded(G)
    f32 = jnp.float32

    pair_rows = rounded(NH * B + G)
    packet_rows = rounded(A * rows + NH * B)
    sizes = (n, npair, A, B, rows, R, group, part)
    vmem = pl.BlockSpec(memory_space=pltpu.VMEM)
    hbm = pl.BlockSpec(memory_space=pl.ANY)
    dma = pltpu.SemaphoreType.DMA

    def scratch(*shape):
        return pltpu.VMEM(shape, f32)

    shapes = tuple(
        jax.ShapeDtypeStruct(x.shape, f32) for x in (gram_field, left_variance, right_variance)
    )
    return pl.pallas_call(
        functools.partial(body, sizes),
        out_shape=shapes,
        in_specs=[hbm] * 4,
        out_specs=(hbm, vmem, vmem),
        scratch_shapes=[
            scratch(A, B, rows + 2, R, W),
            scratch(n, A, part, H, H, width),
            scratch(A, B, rows + 2, R, W),
            scratch(A, B, rows, R, W),
            scratch(B, A, PR, R, W),
            scratch(G, max(A * PR * R, pair_rows + Gp, NH * B + Bp), 128),
            scratch(n, G, A, PR, H, 128),
            scratch(A, H + 2, H, 128),
            scratch(B, NH, A * (PR + 2) * R, 128),
            scratch(A, rows, R, 128),
            scratch(A, H, H, 128),
            scratch(NH * B + G, R, 128),
            scratch(A, B, rows, R, W),
            scratch(n, packet_rows, 128),
            scratch(npair, pair_rows, 128),
            scratch(pair_rows, 128),
            scratch(A, rows, R, 128),
            scratch(A, rows, R, 128),
            scratch(A, H, H, 128),
            scratch(A, H, H, 128),
            scratch(Bp, W),
            scratch(Bp, W),
            scratch(Gp, 128),
            scratch(Gp, 128),
            pltpu.VMEM((group, W, 128), jnp.bfloat16),
            scratch(A, R, 128),
            scratch(R, R, 128),
            scratch(H * R, 128),
            scratch(R * R, 128),
            scratch(A, R, R),
            scratch(B, R, R),
            scratch(Bp, W),
            dma((A + 3,)), dma((A, PR)), dma((2,)), dma((2,)),
            dma((n,)), dma((n,)), dma((n,)), dma((n,)),
            dma((2,)), dma((2,)), dma((n,)), dma((n,)), dma((npair,)), dma((npair,)),
        ],
        compiler_params=pltpu.CompilerParams(
            collective_id=0, has_side_effects=True, vmem_limit_bytes=64 * 1024 * 1024
        ),
        name="arc_reverse",
    )(gram_field, cotangent, left_variance, right_variance)


def solution(mesh):
    in_specs = (
        P("pair", None, "row", None, None),
        P("pair", None, None),
        P(),
        P("pair", "row", None, None, None),
    )
    out_specs = (P("pair", None, "row", None, None), P("pair", None, None), P())
    return jax.shard_map(
        functools.partial(on_device, mesh.shape["row"], mesh.shape["pair"]),
        mesh=mesh, in_specs=in_specs, out_specs=out_specs, check_vma=False,
    )
```

```python
import functools
import math

import jax
import jax.numpy as jnp
from jax import lax
from jax.experimental import pallas as pl
from jax.experimental.pallas import tpu as pltpu
from jax.sharding import PartitionSpec as P

ARCSIN_EVEN = (2.61397078, -1.36807576, 0.342139678, -0.0179491288)
ARCSIN_ROOT = (-1.61397053, 0.727749535, -0.104947558)


def divided(x, k):
    return x >> (k.bit_length() - 1) if k & (k - 1) == 0 else lax.div(x, k)


def left_over(x, k):
    return x & (k - 1) if k & (k - 1) == 0 else lax.rem(x, k)


def lane_of(shape):
    return lax.broadcasted_iota(jnp.int32, shape, len(shape) - 1)


def sub_of(shape):
    return lax.broadcasted_iota(jnp.int32, shape, len(shape) - 2)


def pool_matrix(length, group, t):
    half = length // 2
    shape = (length * length, group * half * half)
    row = sub_of(shape)
    lane = lane_of(shape)
    row_k, row_l = divided(row, length), left_over(row, length)
    lane_t, place = divided(lane, half * half), left_over(lane, half * half)
    same = (
        (lane_t == t)
        & (divided(row_k, 2) == divided(place, half))
        & (divided(row_l, 2) == left_over(place, half))
    )
    return jnp.where(same, 1.0, 0.0).astype(jnp.bfloat16)


def split_dot(x, matrix, dims=((1,), (0,)), terms=2):
    total = None
    for _ in range(terms):
        piece = x.astype(jnp.bfloat16)
        y = lax.dot_general(piece, matrix, (dims, ((), ())), preferred_element_type=jnp.float32)
        total = y if total is None else total + y
        x = x - piece.astype(jnp.float32)
    return total


def arc_parts(rho):
    square = rho * rho
    rest = 1.0 - square
    sine = rest * lax.rsqrt(rest)
    even = ARCSIN_EVEN[3]
    for c in ARCSIN_EVEN[2::-1]:
        even = even * square + c
    root = ARCSIN_ROOT[2]
    for c in ARCSIN_ROOT[1::-1]:
        root = root * square + c
    angle = (0.5 * math.pi) + rho * (even + sine * root)
    return sine, angle


def roll(x, shift, axis):
    return pltpu.roll(x, shift % x.shape[axis], axis)


def lane_masks(shape, side, chunks):
    lane = lane_of(shape)
    sub = sub_of(shape)
    col = left_over(lane, side)
    if chunks > 1:
        k_up, k_down = lane < 128 - side, lane >= side
    else:
        k = left_over(divided(lane, side), side)
        k_up, k_down = k + 1 < side, k >= 1
    l_up, l_down = col + 1 < side, col >= 1
    return k_up, k_down, l_up, l_down, l_up & (sub + 1 < shape[0]), l_down & (sub >= 1)


def shift_k_up(chunks, side, mask):
    rolled = [roll(c, -side, 1) for c in chunks] + [0.0]
    return [jnp.where(mask, rolled[h], rolled[h + 1]) for h in range(len(chunks))]


def shift_k_down(chunks, side, mask):
    rolled = [0.0] + [roll(c, side, 1) for c in chunks]
    return [jnp.where(mask, rolled[h + 1], rolled[h]) for h in range(len(chunks))]


def conv_rows(rows, side, masks):
    k_up, k_down, _, _, v_up, v_down = masks
    out = []
    for i in range(1, len(rows) - 1):
        inner = rows[i]
        if rows[i + 1] is not None:
            inner = [x + y for x, y in zip(inner, shift_k_up(rows[i + 1], side, k_up))]
        if rows[i - 1] is not None:
            inner = [x + y for x, y in zip(inner, shift_k_down(rows[i - 1], side, k_down))]
        done = []
        for x in inner:
            up = jnp.where(v_up, roll(roll(x, -1, 0), -1, 1), 0.0)
            down = jnp.where(v_down, roll(roll(x, 1, 0), 1, 1), 0.0)
            done.append(x + up + down)
        out.append(done)
    return out


def conv_flat(chunks, side, masks):
    k_up, k_down, l_up, l_down, _, _ = masks
    ups = shift_k_up(chunks, side, k_up)
    downs = shift_k_down(chunks, side, k_down)
    out = []
    for x, up, down in zip(chunks, ups, downs):
        x = x + up + down
        x = x + jnp.where(l_up, roll(x, -1, 1), 0.0) + jnp.where(l_down, roll(x, 1, 1), 0.0)
        out.append(x * (1.0 / 9.0))
    return out


def conv_columns(columns):
    count, extent = columns.shape[0], columns.shape[1]
    sub = sub_of((extent, 128))
    out = []
    for i in range(count):
        x = columns[i]
        if i > 0:
            x = x + columns[i - 1]
        if i + 1 < count:
            x = x + columns[i + 1]
        up = jnp.where(sub + 1 < extent, roll(x, -1, 0), 0.0)
        down = jnp.where(sub >= 1, roll(x, 1, 0), 0.0)
        out.append((x + up + down) * (1.0 / 9.0))
    return out


def root_pair(x):
    inverse = lax.rsqrt(x)
    return x * inverse, inverse


def rounded(count):
    return -(-count // 8) * 8


def body(
    sizes,
    gram_hbm, cot_hbm, lv_hbm, rv_hbm,
    out_hbm, left_out, right_out,
    gram, cot, slope, sinem, kp, tmp, pooled, back, fine, wsum, wsum2, racc, out_v, packet, pair_all, pair_packet,
    gl_ref, il_ref, gl2_ref, il2_ref, gr_ref, ir_ref, gr2_ref, ir2_ref, mat_ref, lmap, cols, half_cols, ccol,
    lv_ref, rv_ref, right_flat,
    load_sem, out_sem, halo_send, halo_recv, cot_send, cot_recv, pool_send, pool_recv,
    slope_send, slope_recv, left_send, left_recv, pair_send, pair_recv,
):
    n, npair, A, B, rows, R, group, part = sizes
    H = R // 2
    W = R * R
    NH = W // 128
    G = B // group
    PR = rows // 2
    Bp = rounded(B)
    Gp = rounded(G)
    LR = A * rows
    me = lax.axis_index("row")
    mine = lax.axis_index("pair")
    f32 = jnp.float32

    def chunk(h):
        return slice(h * 128, (h + 1) * 128)

    barrier = pltpu.get_barrier_semaphore()
    for d in range(1, n):
        pl.semaphore_signal(barrier, inc=1, device_id={"row": lax.rem(me + d, n)})

    @pl.loop(1, npair)
    def _(d):
        pl.semaphore_signal(barrier, inc=1, device_id={"pair": lax.rem(mine + d, npair)})

    loads = []
    for a in range(A):
        c = pltpu.make_async_copy(gram_hbm.at[a], gram.at[a, :, pl.ds(1, rows)], load_sem.at[a])
        c.start()
        loads.append(c)
    cot_load = pltpu.make_async_copy(cot_hbm, cot.at[me], load_sem.at[A])
    cot_load.start()
    left_load = pltpu.make_async_copy(lv_hbm, lv_ref, load_sem.at[A + 1])
    left_load.start()
    right_load = pltpu.make_async_copy(rv_hbm, rv_ref, load_sem.at[A + 2])
    right_load.start()

    pl.semaphore_wait(barrier, n - 1 + npair - 1)

    has_low = me > 0
    has_high = me < n - 1
    low = jnp.maximum(me - 1, 0)
    high = jnp.minimum(me + 1, n - 1)

    def halo_up():
        return pltpu.make_async_remote_copy(
            src_ref=gram_hbm.at[:, :, rows - 1], dst_ref=gram.at[:, :, 0],
            send_sem=halo_send.at[0], recv_sem=halo_recv.at[0], device_id={"row": high})

    def halo_down():
        return pltpu.make_async_remote_copy(
            src_ref=gram_hbm.at[:, :, 0], dst_ref=gram.at[:, :, rows + 1],
            send_sem=halo_send.at[1], recv_sem=halo_recv.at[1], device_id={"row": low})

    def slope_up():
        return pltpu.make_async_remote_copy(
            src_ref=slope.at[:, :, rows], dst_ref=slope.at[:, :, 0],
            send_sem=slope_send.at[0], recv_sem=slope_recv.at[0], device_id={"row": high})

    def slope_down():
        return pltpu.make_async_remote_copy(
            src_ref=slope.at[:, :, 1], dst_ref=slope.at[:, :, rows + 1],
            send_sem=slope_send.at[1], recv_sem=slope_recv.at[1], device_id={"row": low})

    def row_copy(ref, sends, recvs, d):
        return pltpu.make_async_remote_copy(
            src_ref=ref.at[me], dst_ref=ref.at[me], send_sem=sends.at[d],
            recv_sem=recvs.at[me], device_id={"row": lax.rem(me + d, n)})

    def row_arrival(ref, sends, recvs, d):
        source = lax.rem(me + d, n)
        return pltpu.make_async_remote_copy(
            src_ref=ref.at[source], dst_ref=ref.at[source], send_sem=sends.at[d],
            recv_sem=recvs.at[source], device_id={"row": source})

    @pl.when(has_high)
    def _():
        halo_up().start()

    @pl.when(has_low)
    def _():
        halo_down().start()

    cot_load.wait()
    for d in range(1, n):
        row_copy(cot, cot_send, cot_recv, d).start()

    zero_row = jnp.zeros((A, B, R, W), f32)

    @pl.when(jnp.logical_not(has_low))
    def _():
        gram[:, :, 0] = zero_row
        slope[:, :, 0] = zero_row

    @pl.when(jnp.logical_not(has_high))
    def _():
        gram[:, :, rows + 1] = zero_row
        slope[:, :, rows + 1] = zero_row

    for t in range(group):
        mat_ref[t] = pool_matrix(R, group, t)
    ones = jnp.ones((128, 128), jnp.bfloat16)
    left_load.wait()
    right_load.wait()
    lmap[...] = jnp.zeros((A, R, 128), f32)
    lmap[:, :, 0:R] = lv_ref[...]
    sub16 = sub_of((R, 128))
    lane16 = lane_of((R, 128))
    band = jnp.abs(sub16 - lane16) <= 1

    @pl.loop(0, A)
    def _(a):
        v = lmap[a]
        v = v + jnp.where(sub16 + 1 < R, roll(v, -1, 0), 0.0) + jnp.where(sub16 >= 1, roll(v, 1, 0), 0.0)
        lines = []
        for i in range(R):
            lines.append(jnp.where(band, jnp.broadcast_to(v[i : i + 1, :], (R, 128)), 0.0))
        spread = split_dot(jnp.concatenate(lines, axis=0), ones, terms=3) * (1.0 / 9.0)
        cols[...] = spread.reshape(R, R, 128)
        for c in range(H):
            half_cols[c * R : (c + 1) * R] = cols[2 * c] + cols[2 * c + 1]
        even = half_cols[pl.ds(0, H * H, stride=2), :]
        odd = half_cols[pl.ds(1, H * H, stride=2), :]
        second = conv_columns(((even + odd) * 0.125).reshape(H, H, 128))
        for i in range(H):
            g2, i2 = root_pair(second[i])
            gl2_ref[a, i] = g2
            il2_ref[a, i] = i2 * (1.0 / 9.0)
        g1, i1 = root_pair(cols[pl.ds(me * rows, rows)])
        gl_ref[a] = g1
        il_ref[a] = i1 * (1.0 / 9.0)

    flat_masks = lane_masks((Bp, 128), R, NH)
    flat_masks2 = lane_masks((Gp, 128), H, 1)
    wide_lane = lane_of((R, W))
    here = divided(wide_lane, R) == sub_of((R, W))
    choose = jnp.where(
        left_over(sub_of((W, 128)), R) == lane_of((W, 128)), 1.0, 0.0
    ).astype(jnp.bfloat16)
    right_flat[...] = jnp.ones((Bp, W), f32)
    for b in range(B):
        lmap[0] = jnp.zeros((R, 128), f32)
        lmap[0, :, 0:R] = rv_ref[b]
        tiled = split_dot(lmap[0], choose, ((1,), (1,)), terms=3)
        right_flat[b : b + 1, :] = jnp.sum(jnp.where(here, tiled, 0.0), axis=0, keepdims=True)
    first_right = conv_flat([right_flat[:, chunk(h)] for h in range(NH)], R, flat_masks)
    for h in range(NH):
        gr_ref[:, chunk(h)], ir_ref[:, chunk(h)] = root_pair(first_right[h])
    first_flat = jnp.concatenate(first_right, axis=1)
    small = [split_dot(first_flat, mat_ref[t], terms=3) for t in range(group)]
    gr2_ref[...] = jnp.ones((Gp, 128), f32)
    for g in range(G):
        line = None
        for t in range(group):
            b = g * group + t
            y = small[t][b : b + 1, :]
            line = y if line is None else line + y
        gr2_ref[g : g + 1, :] = line * 0.125
    (second_right,) = conv_flat([gr2_ref[...]], H, flat_masks2)
    gr2_ref[...], ir2_ref[...] = root_pair(second_right)

    for c in loads:
        c.wait()

    masks = lane_masks((R, 128), R, NH)

    def forward(a, b, p):
        f = [[gram[a, b, 2 * p + t, :, chunk(h)] for h in range(NH)] for t in range(4)]
        source = conv_rows(f, R, masks)
        for h in range(NH):
            total = None
            for t in range(2):
                i = 2 * p + t
                m = gl_ref[a, i] * gr_ref[b : b + 1, chunk(h)]
                rho = source[t][h] * (il_ref[a, i] * ir_ref[b : b + 1, chunk(h)])
                sine, angle = arc_parts(rho)
                sm = m * sine
                slope[a, b, i + 1, :, chunk(h)] = angle
                sinem[a, b, i, :, chunk(h)] = sm
                term = sm + m * (angle * rho)
                total = term if total is None else total + term
            kp[b, a, p, :, chunk(h)] = total

    early = max(PR - 2, 0)

    block = 2 if A % 2 == 0 else 1
    turns = A // block

    def ordered(step):
        q = divided(step, turns)
        p = jnp.where(q < early, q + 1, jnp.where(q == PR - 2, 0, PR - 1))
        return left_over(step, turns) * block, p

    @pl.loop(0, turns * PR)
    def _(step):
        @pl.when(step == early * turns)
        def _():
            @pl.when(has_low)
            def _():
                halo_up().wait_recv()

            @pl.when(has_high)
            def _():
                halo_down().wait_recv()

        a, p = ordered(step)
        for t in range(block):
            for b in range(B):
                forward(a + t, b, p)

    for g in range(G):
        acc = None
        for t in range(group):
            y = split_dot(kp[g * group + t].reshape(A * PR * R, W), mat_ref[t])
            acc = y if acc is None else acc + y
        tmp[g, 0 : A * PR * R] = acc
    for g in range(G):
        even = tmp[g, pl.ds(0, A * PR * H, stride=2), :]
        odd = tmp[g, pl.ds(1, A * PR * H, stride=2), :]
        pooled[me, g] = ((even + odd) * (1.0 / (32.0 * math.pi))).reshape(A, PR, H, 128)
    for d in range(1, n):
        row_copy(pooled, pool_send, pool_recv, d).start()

    @pl.when(has_high)
    def _():
        slope_up().start()

    @pl.when(has_low)
    def _():
        slope_down().start()

    for d in range(1, n):
        row_arrival(cot, cot_send, cot_recv, d).wait_recv()

    masks2 = lane_masks((H, 128), H, 1)
    racc[...] = jnp.zeros((NH * B + G, R, 128), f32)

    for d in range(1, n):
        row_arrival(pooled, pool_send, pool_recv, d).wait_recv()

    scale = 2.0 / (9.0 * 2.0 * math.pi * 16.0) / (18.0 * math.pi)
    zero = jnp.zeros((H, 128), f32)
    for g in range(G):
        sources = []
        for a in range(A):
            f = [None] + [[pooled[i // PR, g, a, i % PR]] for i in range(H)] + [None]
            sources.append(conv_rows(f, H, masks2))
        cts = []
        right2 = None
        for a in range(A):
            ct = [None]
            for i in range(H):
                m = gl2_ref[a, i] * gr2_ref[g : g + 1, :]
                rho = sources[a][i][0] * (il2_ref[a, i] * ir2_ref[g : g + 1, :])
                sine, angle = arc_parts(rho)
                pieces = []
                for t in range(group):
                    b = g * group + t
                    pieces.append(cot[b // part, a, b % part, i])
                c = jnp.concatenate(pieces, axis=1)
                ct.append([c * angle])
                w = c * (m * sine)
                right2 = w if right2 is None else right2 + w
                wsum2[a, i] = w if g == 0 else wsum2[a, i] + w
            ct.append(None)
            cts.append(ct)
        racc[NH * B + g, 0:H] = right2
        for a in range(A):
            b_rows = conv_rows(cts[a], H, masks2)
            back[a, 0] = zero
            back[a, H + 1] = zero
            for i in range(H):
                back[a, i + 1] = b_rows[i][0] * scale
        x = back[:, pl.ds(me * PR, PR + 2)].reshape(A * (PR + 2) * H, 128)
        for t in range(group):
            y = split_dot(x, mat_ref[t], ((1,), (1,)))
            for h in range(NH):
                fine[g * group + t, h, pl.ds(0, A * (PR + 2) * H, stride=2), :] = y[:, chunk(h)]
                fine[g * group + t, h, pl.ds(1, A * (PR + 2) * H, stride=2), :] = y[:, chunk(h)]

    def fine_row(a, b, h, c):
        first = (a * (PR + 2) + c) * R
        if not isinstance(first, int):
            first = pl.multiple_of(first, 8)
        return fine[b, h, pl.ds(first, R), :]

    @pl.loop(0, A)
    def _(a):
        lsum = [None] * rows
        for b in range(B):
            for h in range(NH):
                total = None
                for p in range(PR):
                    bk = fine_row(a, b, h, p + 1)
                    for t in range(2):
                        i = 2 * p + t
                        w = bk * sinem[a, b, i, :, chunk(h)]
                        total = w if total is None else total + w
                        lsum[i] = w if lsum[i] is None else lsum[i] + w
                racc[h * B + b] = racc[h * B + b] + total
        for i in range(rows):
            wsum[a, i] = lsum[i]

    diagonal = (sub16 == lane16)[None]
    sums = split_dot(wsum[...].reshape(LR * R, 128), ones).reshape(LR, R, 128)
    inverse = il_ref[...].reshape(LR, R, 128)
    sums = sums * (inverse * inverse * (2.25 * 81.0))
    packet[me, 0:LR, :] = jnp.sum(jnp.where(diagonal, sums, 0.0), axis=1)
    right_sums = jnp.sum(racc[...], axis=1)
    packet[me, LR : LR + NH * B, :] = right_sums[0 : NH * B]
    for d in range(1, n):
        row_copy(packet, left_send, left_recv, d).start()

    def final(a, b, p):
        f = [
            [fine_row(a, b, h, p + (t + 1) // 2) * slope[a, b, 2 * p + t, :, chunk(h)] for h in range(NH)]
            for t in range(4)
        ]
        value = conv_rows(f, R, masks)
        for t in range(2):
            for h in range(NH):
                out_v[a, b, 2 * p + t, :, chunk(h)] = value[t][h]

    def store(a, p):
        two = pl.ds(2 * p, 2)
        some = pl.ds(a, block)
        return pltpu.make_async_copy(out_v.at[some, :, two], out_hbm.at[some, :, two], out_sem.at[a, p])

    def pair_copy(d):
        return pltpu.make_async_remote_copy(
            src_ref=pair_packet, dst_ref=pair_all.at[mine], send_sem=pair_send.at[d],
            recv_sem=pair_recv.at[mine], device_id={"pair": lax.rem(mine + d, npair)})

    def pair_arrival(d):
        source = lax.rem(mine + d, npair)
        return pltpu.make_async_remote_copy(
            src_ref=pair_packet, dst_ref=pair_all.at[source], send_sem=pair_send.at[d],
            recv_sem=pair_recv.at[source], device_id={"pair": source})

    pair_packet[...] = jnp.zeros(pair_packet.shape, f32)
    pair_packet[NH * B : NH * B + G, :] = right_sums[NH * B : NH * B + G]

    @pl.loop(0, turns * PR)
    def _(step):
        @pl.when(step == early * turns)
        def _():
            for d in range(1, n):
                row_arrival(packet, left_send, left_recv, d).wait_recv()
            right = packet[0, LR : LR + NH * B, :]
            for r in range(1, n):
                right = right + packet[r, LR : LR + NH * B, :]
            pair_packet[0 : NH * B, :] = right
            pair_all[mine] = pair_packet[...]

            @pl.loop(1, npair)
            def _(d):
                pair_copy(d).start()

            @pl.when(has_low)
            def _():
                slope_up().wait_recv()

            @pl.when(has_high)
            def _():
                slope_down().wait_recv()

        a, p = ordered(step)
        for t in range(block):
            for b in range(B):
                final(a + t, b, p)
        store(a, p).start()

    inverse2 = il2_ref[...].reshape(A * H, H, 128)
    sums2 = split_dot(wsum2[...].reshape(A * H * H, 128), ones).reshape(A * H, H, 128)
    sums2 = sums2 * (inverse2 * inverse2 * (81.0 / (4.0 * math.pi * 8.0)))
    wsum2[...] = sums2.reshape(A, H, H, 128)

    @pl.loop(0, A)
    def _(a):
        mixed = conv_columns(wsum2[a])
        for c in range(H):
            for t in range(2):
                ccol[pl.ds((2 * c + t) * R, H, stride=2), :] = mixed[c]
                ccol[pl.ds((2 * c + t) * R + 1, H, stride=2), :] = mixed[c]
        coarse = jnp.sum(jnp.where(diagonal, ccol[...].reshape(R, R, 128), 0.0), axis=1)
        local = jnp.concatenate([packet[r, pl.ds(a * rows, rows), :] for r in range(n)], axis=0)
        v = coarse + local
        v = v + jnp.where(sub16 + 1 < R, roll(v, -1, 0), 0.0) + jnp.where(sub16 >= 1, roll(v, 1, 0), 0.0)
        v = (v + roll(v, 1, 1) + roll(v, -1, 1)) * (1.0 / 9.0)
        left_out[a] = v[:, 0:R]

    @pl.loop(1, npair)
    def _(d):
        pair_arrival(d).wait_recv()
    total = pair_all[0]
    for r in range(1, npair):
        total = total + pair_all[r]
    pair_packet_rows = pair_packet.shape[0]
    tmp[0, 0:pair_packet_rows, :] = total
    tmp[0, pair_packet_rows : pair_packet_rows + Gp, :] = jnp.zeros((Gp, 128), f32)
    coarse = tmp[0, NH * B : NH * B + Gp, :]
    (coarse,) = conv_flat([coarse * (ir2_ref[...] * ir2_ref[...] * (1.0 / (4.0 * math.pi * 8.0)))], H, flat_masks2)
    wide = [split_dot(coarse, mat_ref[t], ((1,), (1,)), terms=3) for t in range(group)]
    right_flat[...] = jnp.zeros((Bp, W), f32)
    for b in range(B):
        right_flat[b : b + 1, :] = wide[b % group][b // group : b // group + 1, :]
    pieces = []
    for h in range(NH):
        scale = ir_ref[:, chunk(h)]
        pieces.append(right_flat[:, chunk(h)] + tmp[0, h * B : h * B + Bp, :] * (scale * scale * 2.25))
    pieces = conv_flat(pieces, R, flat_masks)
    for h in range(NH):
        right_flat[:, chunk(h)] = pieces[h]
    for b in range(B):
        line = jnp.where(here, jnp.broadcast_to(right_flat[b : b + 1, :], (R, W)), 0.0)
        right_out[b] = split_dot(line, choose, terms=3)[:, 0:R]

    @pl.loop(0, turns * PR)
    def _(step):
        a, p = ordered(step)
        store(a, p).wait()

    @pl.when(has_high)
    def _():
        halo_up().wait_send()
        slope_up().wait_send()

    @pl.when(has_low)
    def _():
        halo_down().wait_send()
        slope_down().wait_send()

    for d in range(1, n):
        row_copy(cot, cot_send, cot_recv, d).wait_send()
        row_copy(packet, left_send, left_recv, d).wait_send()
        row_copy(pooled, pool_send, pool_recv, d).wait_send()

    @pl.loop(1, npair)
    def _(d):
        pair_copy(d).wait_send()


def on_device(n, npair, gram_field, left_variance, right_variance, cotangent):
    A, B, rows, R, W = gram_field.shape
    part = cotangent.shape[1]
    H = R // 2
    NH = W // 128
    width = H * H
    group = 128 // width
    G = B // group
    PR = rows // 2
    Bp, Gp = rounded(B), rounded(G)
    f32 = jnp.float32

    pair_rows = rounded(NH * B + G)
    packet_rows = rounded(A * rows + NH * B)
    sizes = (n, npair, A, B, rows, R, group, part)
    vmem = pl.BlockSpec(memory_space=pltpu.VMEM)
    hbm = pl.BlockSpec(memory_space=pl.ANY)
    dma = pltpu.SemaphoreType.DMA

    def scratch(*shape):
        return pltpu.VMEM(shape, f32)

    shapes = tuple(
        jax.ShapeDtypeStruct(x.shape, f32) for x in (gram_field, left_variance, right_variance)
    )
    out, left, right = pl.pallas_call(
        functools.partial(body, sizes),
        out_shape=shapes,
        in_specs=[hbm] * 4,
        out_specs=(hbm, vmem, vmem),
        scratch_shapes=[
            scratch(A, B, rows + 2, R, W),
            scratch(n, A, part, H, H, width),
            scratch(A, B, rows + 2, R, W),
            scratch(A, B, rows, R, W),
            scratch(B, A, PR, R, W),
            scratch(G, max(A * PR * R, pair_rows + Gp, NH * B + Bp), 128),
            scratch(n, G, A, PR, H, 128),
            scratch(A, H + 2, H, 128),
            scratch(B, NH, A * (PR + 2) * R, 128),
            scratch(A, rows, R, 128),
            scratch(A, H, H, 128),
            scratch(NH * B + G, R, 128),
            scratch(A, B, rows, R, W),
            scratch(n, packet_rows, 128),
            scratch(npair, pair_rows, 128),
            scratch(pair_rows, 128),
            scratch(A, rows, R, 128),
            scratch(A, rows, R, 128),
            scratch(A, H, H, 128),
            scratch(A, H, H, 128),
            scratch(Bp, W),
            scratch(Bp, W),
            scratch(Gp, 128),
            scratch(Gp, 128),
            pltpu.VMEM((group, W, 128), jnp.bfloat16),
            scratch(A, R, 128),
            scratch(R, R, 128),
            scratch(H * R, 128),
            scratch(R * R, 128),
            scratch(A, R, R),
            scratch(B, R, R),
            scratch(Bp, W),
            dma((A + 3,)), dma((A, PR)), dma((2,)), dma((2,)),
            dma((n,)), dma((n,)), dma((n,)), dma((n,)),
            dma((2,)), dma((2,)), dma((n,)), dma((n,)), dma((npair,)), dma((npair,)),
        ],
        compiler_params=pltpu.CompilerParams(
            collective_id=0, has_side_effects=True, vmem_limit_bytes=64 * 1024 * 1024
        ),
        name="arc_reverse",
    )(gram_field, cotangent, left_variance, right_variance)
    return out * 0.5, left, right


def solution(mesh):
    in_specs = (
        P("pair", None, "row", None, None),
        P("pair", None, None),
        P(),
        P("pair", "row", None, None, None),
    )
    out_specs = (P("pair", None, "row", None, None), P("pair", None, None), P())
    return jax.shard_map(
        functools.partial(on_device, mesh.shape["row"], mesh.shape["pair"]),
        mesh=mesh, in_specs=in_specs, out_specs=out_specs, check_vma=False,
    )
```

```python
import functools
import math

import jax
import jax.numpy as jnp
from jax import lax
from jax.experimental import pallas as pl
from jax.experimental.pallas import tpu as pltpu
from jax.sharding import PartitionSpec as P

ARCSIN_EVEN = (2.61397078, -1.36807576, 0.342139678, -0.0179491288)
ARCSIN_ROOT = (-1.61397053, 0.727749535, -0.104947558)


def divided(x, k):
    return x >> (k.bit_length() - 1) if k & (k - 1) == 0 else lax.div(x, k)


def left_over(x, k):
    return x & (k - 1) if k & (k - 1) == 0 else lax.rem(x, k)


def lane_of(shape):
    return lax.broadcasted_iota(jnp.int32, shape, len(shape) - 1)


def sub_of(shape):
    return lax.broadcasted_iota(jnp.int32, shape, len(shape) - 2)


def pool_matrix(length, group, t):
    half = length // 2
    shape = (length * length, group * half * half)
    row = sub_of(shape)
    lane = lane_of(shape)
    row_k, row_l = divided(row, length), left_over(row, length)
    lane_t, place = divided(lane, half * half), left_over(lane, half * half)
    same = (
        (lane_t == t)
        & (divided(row_k, 2) == divided(place, half))
        & (divided(row_l, 2) == left_over(place, half))
    )
    return jnp.where(same, 1.0, 0.0).astype(jnp.bfloat16)


def split_dot(x, matrix, dims=((1,), (0,)), terms=2):
    total = None
    for _ in range(terms):
        piece = x.astype(jnp.bfloat16)
        y = lax.dot_general(piece, matrix, (dims, ((), ())), preferred_element_type=jnp.float32)
        total = y if total is None else total + y
        x = x - piece.astype(jnp.float32)
    return total


def arc_parts(rho):
    square = rho * rho
    rest = 1.0 - square
    sine = rest * lax.rsqrt(rest)
    even = ARCSIN_EVEN[3]
    for c in ARCSIN_EVEN[2::-1]:
        even = even * square + c
    root = ARCSIN_ROOT[2]
    for c in ARCSIN_ROOT[1::-1]:
        root = root * square + c
    angle = (0.5 * math.pi) + rho * (even + sine * root)
    return sine, angle


def roll(x, shift, axis):
    return pltpu.roll(x, shift % x.shape[axis], axis)


def lane_masks(shape, side, chunks):
    lane = lane_of(shape)
    sub = sub_of(shape)
    col = left_over(lane, side)
    if chunks > 1:
        k_up, k_down = lane < 128 - side, lane >= side
    else:
        k = left_over(divided(lane, side), side)
        k_up, k_down = k + 1 < side, k >= 1
    l_up, l_down = col + 1 < side, col >= 1
    return k_up, k_down, l_up, l_down, l_up & (sub + 1 < shape[0]), l_down & (sub >= 1)


def shift_k_up(chunks, side, mask):
    rolled = [roll(c, -side, 1) for c in chunks] + [0.0]
    return [jnp.where(mask, rolled[h], rolled[h + 1]) for h in range(len(chunks))]


def shift_k_down(chunks, side, mask):
    rolled = [0.0] + [roll(c, side, 1) for c in chunks]
    return [jnp.where(mask, rolled[h + 1], rolled[h]) for h in range(len(chunks))]


def conv_rows(rows, side, masks):
    k_up, k_down, _, _, v_up, v_down = masks
    out = []
    for i in range(1, len(rows) - 1):
        inner = rows[i]
        if rows[i + 1] is not None:
            inner = [x + y for x, y in zip(inner, shift_k_up(rows[i + 1], side, k_up))]
        if rows[i - 1] is not None:
            inner = [x + y for x, y in zip(inner, shift_k_down(rows[i - 1], side, k_down))]
        done = []
        for x in inner:
            up = jnp.where(v_up, roll(roll(x, -1, 0), -1, 1), 0.0)
            down = jnp.where(v_down, roll(roll(x, 1, 0), 1, 1), 0.0)
            done.append(x + up + down)
        out.append(done)
    return out


def conv_flat(chunks, side, masks):
    k_up, k_down, l_up, l_down, _, _ = masks
    ups = shift_k_up(chunks, side, k_up)
    downs = shift_k_down(chunks, side, k_down)
    out = []
    for x, up, down in zip(chunks, ups, downs):
        x = x + up + down
        x = x + jnp.where(l_up, roll(x, -1, 1), 0.0) + jnp.where(l_down, roll(x, 1, 1), 0.0)
        out.append(x * (1.0 / 9.0))
    return out


def conv_columns(columns):
    count, extent = columns.shape[0], columns.shape[1]
    sub = sub_of((extent, 128))
    out = []
    for i in range(count):
        x = columns[i]
        if i > 0:
            x = x + columns[i - 1]
        if i + 1 < count:
            x = x + columns[i + 1]
        up = jnp.where(sub + 1 < extent, roll(x, -1, 0), 0.0)
        down = jnp.where(sub >= 1, roll(x, 1, 0), 0.0)
        out.append((x + up + down) * (1.0 / 9.0))
    return out


def root_pair(x):
    inverse = lax.rsqrt(x)
    return x * inverse, inverse


def rounded(count):
    return -(-count // 8) * 8


def body(
    sizes,
    gram_hbm, cot_hbm, maps_hbm,
    out_v, left_out, right_out,
    gram, cot, slope, sinem, kp, tmp, pooled, back, fine, wsum, wsum2, racc, packet, pair_all, pair_packet,
    gl_ref, il_ref, gl2_ref, il2_ref, gr_ref, ir_ref, gr2_ref, ir2_ref, mat_ref, lmap, cols, half_cols, ccol,
    lv_ref, rv_ref, right_flat,
    load_sem, halo_send, halo_recv, cot_send, cot_recv, pool_send, pool_recv,
    slope_send, slope_recv, left_send, left_recv, pair_send, pair_recv,
):
    n, npair, A, B, rows, R, group, part = sizes
    H = R // 2
    W = R * R
    NH = W // 128
    G = B // group
    PR = rows // 2
    Bp = rounded(B)
    Gp = rounded(G)
    LR = A * rows
    me = lax.axis_index("row")
    mine = lax.axis_index("pair")
    f32 = jnp.float32

    def chunk(h):
        return slice(h * 128, (h + 1) * 128)

    barrier = pltpu.get_barrier_semaphore()
    for d in range(1, n):
        pl.semaphore_signal(barrier, inc=1, device_id={"row": lax.rem(me + d, n)})

    @pl.loop(1, npair)
    def _(d):
        pl.semaphore_signal(barrier, inc=1, device_id={"pair": lax.rem(mine + d, npair)})

    loads = []
    for a in range(A):
        c = pltpu.make_async_copy(gram_hbm.at[a], gram.at[a, :, pl.ds(1, rows)], load_sem.at[a])
        c.start()
        loads.append(c)
    cot_load = pltpu.make_async_copy(cot_hbm, cot.at[me], load_sem.at[A])
    cot_load.start()
    left_load = pltpu.make_async_copy(maps_hbm.at[pl.ds(0, A)], lv_ref, load_sem.at[A + 1])
    left_load.start()
    right_load = pltpu.make_async_copy(maps_hbm.at[pl.ds(A, B)], rv_ref, load_sem.at[A + 2])
    right_load.start()

    pl.semaphore_wait(barrier, n - 1 + npair - 1)

    has_low = me > 0
    has_high = me < n - 1
    low = jnp.maximum(me - 1, 0)
    high = jnp.minimum(me + 1, n - 1)

    def halo_up():
        return pltpu.make_async_remote_copy(
            src_ref=gram_hbm.at[:, :, rows - 1], dst_ref=gram.at[:, :, 0],
            send_sem=halo_send.at[0], recv_sem=halo_recv.at[0], device_id={"row": high})

    def halo_down():
        return pltpu.make_async_remote_copy(
            src_ref=gram_hbm.at[:, :, 0], dst_ref=gram.at[:, :, rows + 1],
            send_sem=halo_send.at[1], recv_sem=halo_recv.at[1], device_id={"row": low})

    def slope_up():
        return pltpu.make_async_remote_copy(
            src_ref=slope.at[:, :, rows], dst_ref=slope.at[:, :, 0],
            send_sem=slope_send.at[0], recv_sem=slope_recv.at[0], device_id={"row": high})

    def slope_down():
        return pltpu.make_async_remote_copy(
            src_ref=slope.at[:, :, 1], dst_ref=slope.at[:, :, rows + 1],
            send_sem=slope_send.at[1], recv_sem=slope_recv.at[1], device_id={"row": low})

    def row_copy(ref, sends, recvs, d):
        return pltpu.make_async_remote_copy(
            src_ref=ref.at[me], dst_ref=ref.at[me], send_sem=sends.at[d],
            recv_sem=recvs.at[me], device_id={"row": lax.rem(me + d, n)})

    def row_arrival(ref, sends, recvs, d):
        source = lax.rem(me + d, n)
        return pltpu.make_async_remote_copy(
            src_ref=ref.at[source], dst_ref=ref.at[source], send_sem=sends.at[d],
            recv_sem=recvs.at[source], device_id={"row": source})

    @pl.when(has_high)
    def _():
        halo_up().start()

    @pl.when(has_low)
    def _():
        halo_down().start()

    cot_load.wait()
    for d in range(1, n):
        row_copy(cot, cot_send, cot_recv, d).start()

    zero_row = jnp.zeros((A, B, R, W), f32)

    @pl.when(jnp.logical_not(has_low))
    def _():
        gram[:, :, 0] = zero_row
        slope[:, :, 0] = zero_row

    @pl.when(jnp.logical_not(has_high))
    def _():
        gram[:, :, rows + 1] = zero_row
        slope[:, :, rows + 1] = zero_row

    for t in range(group):
        mat_ref[t] = pool_matrix(R, group, t)
    ones = jnp.ones((128, 128), jnp.bfloat16)
    left_load.wait()
    right_load.wait()
    lmap[...] = jnp.zeros((A, R, 128), f32)
    lmap[:, :, 0:R] = lv_ref[...]
    sub16 = sub_of((R, 128))
    lane16 = lane_of((R, 128))
    band = jnp.abs(sub16 - lane16) <= 1

    @pl.loop(0, A)
    def _(a):
        v = lmap[a]
        v = v + jnp.where(sub16 + 1 < R, roll(v, -1, 0), 0.0) + jnp.where(sub16 >= 1, roll(v, 1, 0), 0.0)
        lines = []
        for i in range(R):
            lines.append(jnp.where(band, jnp.broadcast_to(v[i : i + 1, :], (R, 128)), 0.0))
        spread = split_dot(jnp.concatenate(lines, axis=0), ones, terms=3) * (1.0 / 9.0)
        cols[...] = spread.reshape(R, R, 128)
        for c in range(H):
            half_cols[c * R : (c + 1) * R] = cols[2 * c] + cols[2 * c + 1]
        even = half_cols[pl.ds(0, H * H, stride=2), :]
        odd = half_cols[pl.ds(1, H * H, stride=2), :]
        second = conv_columns(((even + odd) * 0.125).reshape(H, H, 128))
        for i in range(H):
            g2, i2 = root_pair(second[i])
            gl2_ref[a, i] = g2
            il2_ref[a, i] = i2 * (1.0 / 9.0)
        g1, i1 = root_pair(cols[pl.ds(me * rows, rows)])
        gl_ref[a] = g1
        il_ref[a] = i1 * (1.0 / 9.0)

    flat_masks = lane_masks((Bp, 128), R, NH)
    flat_masks2 = lane_masks((Gp, 128), H, 1)
    wide_lane = lane_of((R, W))
    here = divided(wide_lane, R) == sub_of((R, W))
    choose = jnp.where(
        left_over(sub_of((W, 128)), R) == lane_of((W, 128)), 1.0, 0.0
    ).astype(jnp.bfloat16)
    right_flat[...] = jnp.ones((Bp, W), f32)
    for b in range(B):
        lmap[0] = jnp.zeros((R, 128), f32)
        lmap[0, :, 0:R] = rv_ref[b]
        tiled = split_dot(lmap[0], choose, ((1,), (1,)), terms=3)
        right_flat[b : b + 1, :] = jnp.sum(jnp.where(here, tiled, 0.0), axis=0, keepdims=True)
    first_right = conv_flat([right_flat[:, chunk(h)] for h in range(NH)], R, flat_masks)
    for h in range(NH):
        gr_ref[:, chunk(h)], ir_ref[:, chunk(h)] = root_pair(first_right[h])
    first_flat = jnp.concatenate(first_right, axis=1)
    small = [split_dot(first_flat, mat_ref[t], terms=3) for t in range(group)]
    gr2_ref[...] = jnp.ones((Gp, 128), f32)
    for g in range(G):
        line = None
        for t in range(group):
            b = g * group + t
            y = small[t][b : b + 1, :]
            line = y if line is None else line + y
        gr2_ref[g : g + 1, :] = line * 0.125
    (second_right,) = conv_flat([gr2_ref[...]], H, flat_masks2)
    gr2_ref[...], ir2_ref[...] = root_pair(second_right)

    for c in loads:
        c.wait()

    masks = lane_masks((R, 128), R, NH)

    def forward(a, b, p):
        f = [[gram[a, b, 2 * p + t, :, chunk(h)] for h in range(NH)] for t in range(4)]
        source = conv_rows(f, R, masks)
        for h in range(NH):
            total = None
            for t in range(2):
                i = 2 * p + t
                m = gl_ref[a, i] * gr_ref[b : b + 1, chunk(h)]
                rho = source[t][h] * (il_ref[a, i] * ir_ref[b : b + 1, chunk(h)])
                sine, angle = arc_parts(rho)
                sm = m * sine
                slope[a, b, i + 1, :, chunk(h)] = angle
                sinem[a, b, i, :, chunk(h)] = sm
                term = sm + m * (angle * rho)
                total = term if total is None else total + term
            kp[b, a, p, :, chunk(h)] = total

    early = max(PR - 2, 0)

    block = 2 if A % 2 == 0 else 1
    turns = A // block

    def ordered(step):
        q = divided(step, turns)
        p = jnp.where(q < early, q + 1, jnp.where(q == PR - 2, 0, PR - 1))
        return left_over(step, turns) * block, p

    @pl.loop(0, turns * PR)
    def _(step):
        @pl.when(step == early * turns)
        def _():
            @pl.when(has_low)
            def _():
                halo_up().wait_recv()

            @pl.when(has_high)
            def _():
                halo_down().wait_recv()

        a, p = ordered(step)
        for t in range(block):
            for b in range(B):
                forward(a + t, b, p)

    for g in range(G):
        acc = None
        for t in range(group):
            y = split_dot(kp[g * group + t].reshape(A * PR * R, W), mat_ref[t])
            acc = y if acc is None else acc + y
        tmp[g, 0 : A * PR * R] = acc
    for g in range(G):
        even = tmp[g, pl.ds(0, A * PR * H, stride=2), :]
        odd = tmp[g, pl.ds(1, A * PR * H, stride=2), :]
        pooled[me, g] = ((even + odd) * (1.0 / (32.0 * math.pi))).reshape(A, PR, H, 128)
    for d in range(1, n):
        row_copy(pooled, pool_send, pool_recv, d).start()

    @pl.when(has_high)
    def _():
        slope_up().start()

    @pl.when(has_low)
    def _():
        slope_down().start()

    for d in range(1, n):
        row_arrival(cot, cot_send, cot_recv, d).wait_recv()

    masks2 = lane_masks((H, 128), H, 1)
    racc[...] = jnp.zeros((NH * B + G, R, 128), f32)

    for d in range(1, n):
        row_arrival(pooled, pool_send, pool_recv, d).wait_recv()

    scale = 1.0 / (9.0 * 2.0 * math.pi * 16.0) / (18.0 * math.pi)
    zero = jnp.zeros((H, 128), f32)
    for g in range(G):
        sources = []
        for a in range(A):
            f = [None] + [[pooled[i // PR, g, a, i % PR]] for i in range(H)] + [None]
            sources.append(conv_rows(f, H, masks2))
        cts = []
        right2 = None
        for a in range(A):
            ct = [None]
            for i in range(H):
                m = gl2_ref[a, i] * gr2_ref[g : g + 1, :]
                rho = sources[a][i][0] * (il2_ref[a, i] * ir2_ref[g : g + 1, :])
                sine, angle = arc_parts(rho)
                pieces = []
                for t in range(group):
                    b = g * group + t
                    pieces.append(cot[b // part, a, b % part, i])
                c = jnp.concatenate(pieces, axis=1)
                ct.append([c * angle])
                w = c * (m * sine)
                right2 = w if right2 is None else right2 + w
                wsum2[a, i] = w if g == 0 else wsum2[a, i] + w
            ct.append(None)
            cts.append(ct)
        racc[NH * B + g, 0:H] = right2
        for a in range(A):
            b_rows = conv_rows(cts[a], H, masks2)
            back[a, 0] = zero
            back[a, H + 1] = zero
            for i in range(H):
                back[a, i + 1] = b_rows[i][0] * scale
        x = back[:, pl.ds(me * PR, PR + 2)].reshape(A * (PR + 2) * H, 128)
        for t in range(group):
            y = split_dot(x, mat_ref[t], ((1,), (1,)))
            for h in range(NH):
                fine[g * group + t, h, pl.ds(0, A * (PR + 2) * H, stride=2), :] = y[:, chunk(h)]
                fine[g * group + t, h, pl.ds(1, A * (PR + 2) * H, stride=2), :] = y[:, chunk(h)]

    def fine_row(a, b, h, c):
        first = (a * (PR + 2) + c) * R
        if not isinstance(first, int):
            first = pl.multiple_of(first, 8)
        return fine[b, h, pl.ds(first, R), :]

    @pl.loop(0, A)
    def _(a):
        lsum = [None] * rows
        for b in range(B):
            for h in range(NH):
                total = None
                for p in range(PR):
                    bk = fine_row(a, b, h, p + 1)
                    for t in range(2):
                        i = 2 * p + t
                        w = bk * sinem[a, b, i, :, chunk(h)]
                        total = w if total is None else total + w
                        lsum[i] = w if lsum[i] is None else lsum[i] + w
                racc[h * B + b] = racc[h * B + b] + total
        for i in range(rows):
            wsum[a, i] = lsum[i]

    diagonal = (sub16 == lane16)[None]
    sums = split_dot(wsum[...].reshape(LR * R, 128), ones).reshape(LR, R, 128)
    inverse = il_ref[...].reshape(LR, R, 128)
    sums = sums * (inverse * inverse * (4.5 * 81.0))
    packet[me, 0:LR, :] = jnp.sum(jnp.where(diagonal, sums, 0.0), axis=1)
    right_sums = jnp.sum(racc[...], axis=1)
    packet[me, LR : LR + NH * B, :] = right_sums[0 : NH * B]
    for d in range(1, n):
        row_copy(packet, left_send, left_recv, d).start()

    def final(a, b, p):
        f = [
            [fine_row(a, b, h, p + (t + 1) // 2) * slope[a, b, 2 * p + t, :, chunk(h)] for h in range(NH)]
            for t in range(4)
        ]
        value = conv_rows(f, R, masks)
        for t in range(2):
            for h in range(NH):
                out_v[a, b, 2 * p + t, :, chunk(h)] = value[t][h]

    def pair_copy(d):
        return pltpu.make_async_remote_copy(
            src_ref=pair_packet, dst_ref=pair_all.at[mine], send_sem=pair_send.at[d],
            recv_sem=pair_recv.at[mine], device_id={"pair": lax.rem(mine + d, npair)})

    def pair_arrival(d):
        source = lax.rem(mine + d, npair)
        return pltpu.make_async_remote_copy(
            src_ref=pair_packet, dst_ref=pair_all.at[source], send_sem=pair_send.at[d],
            recv_sem=pair_recv.at[source], device_id={"pair": source})

    pair_packet[...] = jnp.zeros(pair_packet.shape, f32)
    pair_packet[NH * B : NH * B + G, :] = right_sums[NH * B : NH * B + G]

    @pl.loop(0, turns * PR)
    def _(step):
        @pl.when(step == early * turns)
        def _():
            for d in range(1, n):
                row_arrival(packet, left_send, left_recv, d).wait_recv()
            right = packet[0, LR : LR + NH * B, :]
            for r in range(1, n):
                right = right + packet[r, LR : LR + NH * B, :]
            pair_packet[0 : NH * B, :] = right
            pair_all[mine] = pair_packet[...]

            @pl.loop(1, npair)
            def _(d):
                pair_copy(d).start()

            @pl.when(has_low)
            def _():
                slope_up().wait_recv()

            @pl.when(has_high)
            def _():
                slope_down().wait_recv()

        a, p = ordered(step)
        for t in range(block):
            for b in range(B):
                final(a + t, b, p)

    inverse2 = il2_ref[...].reshape(A * H, H, 128)
    sums2 = split_dot(wsum2[...].reshape(A * H * H, 128), ones).reshape(A * H, H, 128)
    sums2 = sums2 * (inverse2 * inverse2 * (81.0 / (4.0 * math.pi * 8.0)))
    wsum2[...] = sums2.reshape(A, H, H, 128)

    @pl.loop(0, A)
    def _(a):
        mixed = conv_columns(wsum2[a])
        for c in range(H):
            for t in range(2):
                ccol[pl.ds((2 * c + t) * R, H, stride=2), :] = mixed[c]
                ccol[pl.ds((2 * c + t) * R + 1, H, stride=2), :] = mixed[c]
        coarse = jnp.sum(jnp.where(diagonal, ccol[...].reshape(R, R, 128), 0.0), axis=1)
        local = jnp.concatenate([packet[r, pl.ds(a * rows, rows), :] for r in range(n)], axis=0)
        v = coarse + local
        v = v + jnp.where(sub16 + 1 < R, roll(v, -1, 0), 0.0) + jnp.where(sub16 >= 1, roll(v, 1, 0), 0.0)
        v = (v + roll(v, 1, 1) + roll(v, -1, 1)) * (1.0 / 9.0)
        left_out[a] = v[:, 0:R]

    @pl.loop(1, npair)
    def _(d):
        pair_arrival(d).wait_recv()
    total = pair_all[0]
    for r in range(1, npair):
        total = total + pair_all[r]
    pair_packet_rows = pair_packet.shape[0]
    tmp[0, 0:pair_packet_rows, :] = total
    tmp[0, pair_packet_rows : pair_packet_rows + Gp, :] = jnp.zeros((Gp, 128), f32)
    coarse = tmp[0, NH * B : NH * B + Gp, :]
    (coarse,) = conv_flat([coarse * (ir2_ref[...] * ir2_ref[...] * (1.0 / (4.0 * math.pi * 8.0)))], H, flat_masks2)
    wide = [split_dot(coarse, mat_ref[t], ((1,), (1,)), terms=3) for t in range(group)]
    right_flat[...] = jnp.zeros((Bp, W), f32)
    for b in range(B):
        right_flat[b : b + 1, :] = wide[b % group][b // group : b // group + 1, :]
    pieces = []
    for h in range(NH):
        scale = ir_ref[:, chunk(h)]
        pieces.append(right_flat[:, chunk(h)] + tmp[0, h * B : h * B + Bp, :] * (scale * scale * 4.5))
    pieces = conv_flat(pieces, R, flat_masks)
    for h in range(NH):
        right_flat[:, chunk(h)] = pieces[h]
    for b in range(B):
        line = jnp.where(here, jnp.broadcast_to(right_flat[b : b + 1, :], (R, W)), 0.0)
        right_out[b] = split_dot(line, choose, terms=3)[:, 0:R]

    @pl.when(has_high)
    def _():
        halo_up().wait_send()
        slope_up().wait_send()

    @pl.when(has_low)
    def _():
        halo_down().wait_send()
        slope_down().wait_send()

    for d in range(1, n):
        row_copy(cot, cot_send, cot_recv, d).wait_send()
        row_copy(packet, left_send, left_recv, d).wait_send()
        row_copy(pooled, pool_send, pool_recv, d).wait_send()

    @pl.loop(1, npair)
    def _(d):
        pair_copy(d).wait_send()


def on_device(n, npair, gram_field, left_variance, right_variance, cotangent):
    A, B, rows, R, W = gram_field.shape
    part = cotangent.shape[1]
    H = R // 2
    NH = W // 128
    width = H * H
    group = 128 // width
    G = B // group
    PR = rows // 2
    Bp, Gp = rounded(B), rounded(G)
    f32 = jnp.float32

    pair_rows = rounded(NH * B + G)
    packet_rows = rounded(A * rows + NH * B)
    sizes = (n, npair, A, B, rows, R, group, part)
    vmem = pl.BlockSpec(memory_space=pltpu.VMEM)
    hbm = pl.BlockSpec(memory_space=pl.ANY)
    dma = pltpu.SemaphoreType.DMA

    def scratch(*shape):
        return pltpu.VMEM(shape, f32)

    shapes = tuple(
        jax.ShapeDtypeStruct(x.shape, f32) for x in (gram_field, left_variance, right_variance)
    )
    return pl.pallas_call(
        functools.partial(body, sizes),
        out_shape=shapes,
        in_specs=[hbm] * 3,
        out_specs=(vmem, vmem, vmem),
        scratch_shapes=[
            scratch(A, B, rows + 2, R, W),
            scratch(n, A, part, H, H, width),
            scratch(A, B, rows + 2, R, W),
            scratch(A, B, rows, R, W),
            scratch(B, A, PR, R, W),
            scratch(G, max(A * PR * R, pair_rows + Gp, NH * B + Bp), 128),
            scratch(n, G, A, PR, H, 128),
            scratch(A, H + 2, H, 128),
            scratch(B, NH, A * (PR + 2) * R, 128),
            scratch(A, rows, R, 128),
            scratch(A, H, H, 128),
            scratch(NH * B + G, R, 128),
            scratch(n, packet_rows, 128),
            scratch(npair, pair_rows, 128),
            scratch(pair_rows, 128),
            scratch(A, rows, R, 128),
            scratch(A, rows, R, 128),
            scratch(A, H, H, 128),
            scratch(A, H, H, 128),
            scratch(Bp, W),
            scratch(Bp, W),
            scratch(Gp, 128),
            scratch(Gp, 128),
            pltpu.VMEM((group, W, 128), jnp.bfloat16),
            scratch(A, R, 128),
            scratch(R, R, 128),
            scratch(H * R, 128),
            scratch(R * R, 128),
            scratch(A, R, R),
            scratch(B, R, R),
            scratch(Bp, W),
            dma((A + 3,)), dma((2,)), dma((2,)),
            dma((n,)), dma((n,)), dma((n,)), dma((n,)),
            dma((2,)), dma((2,)), dma((n,)), dma((n,)), dma((npair,)), dma((npair,)),
        ],
        compiler_params=pltpu.CompilerParams(
            collective_id=0, has_side_effects=True, vmem_limit_bytes=int(52 * 2**20)
        ),
        name="arc_reverse",
    )(gram_field, cotangent, jnp.concatenate([left_variance, right_variance], axis=0))


def solution(mesh):
    in_specs = (
        P("pair", None, "row", None, None),
        P("pair", None, None),
        P(),
        P("pair", "row", None, None, None),
    )
    out_specs = (P("pair", None, "row", None, None), P("pair", None, None), P())
    return jax.shard_map(
        functools.partial(on_device, mesh.shape["row"], mesh.shape["pair"]),
        mesh=mesh, in_specs=in_specs, out_specs=out_specs, check_vma=False,
    )
```
